512 devices in a mesh: dom: 128 (over z, y, core), field: 4 (over x).
Axes of the slice: x: 4, y: 8, z: 8, core: 2. Of those that a mesh axis runs over, the one named last changes fastest.
Arguments:
- traces: float32 [8, 28, 65536], P('field', None, 'dom'), may hold values from -6 to 6
- interior_source: bfloat16 [8, 84, 32768], P('field', None, 'dom'), may hold values from -6 to 6
- orders: int32 [32768], P('dom'), may hold values from 2 to 6, as said below
- element_scale: float32 [32768], P('dom'), may hold values from 0.5 to 2
- element_faces: int32 [4, 32768], P(None, 'dom'), may hold values from 0 to 65535, as said below
- solver_slots: int32 [65536], P('dom'), may hold values from 0 to 511, as said below
- line_diagonal: float32 [8, 65536], P('field', 'dom'), may hold values from 2.5 to 6
- species_mix: float32 [8, 8], P('field'), may hold values from -3 to 3
- couple_in: bfloat16 [672, 896], P('field'), may hold values from -0.1875 to 0.1875
- local_inverse: bfloat16 [672, 672], P('field'), may hold values from -0.25 to 0.25
- trace_block: bfloat16 [896, 896], P('field'), may hold values from -0.1875 to 0.1875
- couple_out: bfloat16 [896, 672], P('field'), may hold values from -0.25 to 0.25
Outputs:
- new_traces: float32 [8, 28, 65536], P('field', None, 'dom')
- mixed: float32 [8, 28, 65536], P('field', None, 'dom')
The draws below stay inside these ranges and needn't reach their ends.
Inputs may be any that keep to these rules, and one draw needn't show every extreme that they name: `element_faces`: each face is named by exactly two (element, face) entries. The elements of partition d name the faces owned by d, the last 32 faces of partition d - 1 and the first 32 faces of partition d + 1, with partitions counted cyclically. `orders`: orders are higher on some partitions than on others. `solver_slots`: each partition's 512 entries are a permutation of 0 to 511.
All inputs are finite; a program needn't handle non-finite values.
Results may differ from the reference program's by a relative error of at most 0.0029.
The reference program's roundings to bfloat16 on the way (of `gathered`, `loads` and `interior`) count: a program that leaves them out, or rounds other values in their place, can miss the bound.
Values may be sent and summed in bfloat16 or wider, within the bound.
A program may use at most 64 MiB of HBM per device.

```python
import math
import jax
import jax.numpy as jnp
from jax import lax

NCOMP = 8
NFD = 28
NID = 84
DEG = 3
E_DEV = 256
FACE_DEV = 512
RIM = 32
ELEMS = 32768
NFACE = 65536
N_DOM = 128


def faces_of_partition(part_index, key):
    base = part_index * FACE_DEV
    inner_ids = jnp.arange(RIM, FACE_DEV - RIM, dtype=jnp.int32)
    first_ids = jnp.arange(0, RIM, dtype=jnp.int32)
    last_ids = jnp.arange(FACE_DEV - RIM, FACE_DEV, dtype=jnp.int32)
    next_base = (part_index + 1) % N_DOM * FACE_DEV
    prev_base = (part_index + N_DOM - 1) % N_DOM * FACE_DEV
    listed = jnp.concatenate([base + inner_ids, base + inner_ids, base + first_ids, base + last_ids, next_base + first_ids, prev_base + last_ids])
    order = jax.random.permutation(jax.random.fold_in(key, part_index), 4 * E_DEV)
    return listed[order].reshape(E_DEV, 4).T


def draw_element_faces(key, part):
    indices = jnp.arange(N_DOM, dtype=jnp.int32)
    blocks = jax.vmap(faces_of_partition, in_axes=(0, None))(indices, jax.random.fold_in(key, 11))
    return jnp.transpose(blocks, (1, 0, 2)).reshape(4, ELEMS).astype(jnp.int32)


def slots_of_partition(part_index, key):
    return jax.random.permutation(jax.random.fold_in(key, part_index), FACE_DEV).astype(jnp.int32)


def draw_solver_slots(key, part):
    indices = jnp.arange(N_DOM, dtype=jnp.int32)
    blocks = jax.vmap(slots_of_partition, in_axes=(0, None))(indices, jax.random.fold_in(key, 23))
    return blocks.reshape(NFACE).astype(jnp.int32)


def draw_orders(key, part):
    bias_key = jax.random.fold_in(key, 31)
    each_key = jax.random.fold_in(key, 37)
    bias = jax.random.randint(bias_key, (N_DOM, 1), 0, 3)
    spread = jax.random.randint(each_key, (N_DOM, E_DEV), 0, 4)
    levels = jnp.minimum(6, 2 + spread + bias).reshape(ELEMS)
    levels = levels.at[0].set(6).at[1].set(2)
    return levels.astype(jnp.int32)


def block_levels(stream_key, extent, shards, least, largest):
    def one(position, shards_of):
        draws = jax.random.uniform(jax.random.fold_in(jax.random.fold_in(stream_key, 6), position), (shards_of,), jnp.float32, least / len(shards), largest / len(shards))
        return jnp.repeat(jnp.exp(draws), extent[position] // shards_of).reshape((-1,) + (1,) * (len(extent) - position - 1))

    gain = one(*shards[0])
    for cut in shards[1:]:
        gain = gain * one(*cut)
    return gain


def normal_values(stream_key, shape, width, bound, split=(), held_as=jnp.bfloat16):
    result = width * jax.random.normal(stream_key, shape, jnp.float32)
    if split:
        result = result * block_levels(stream_key, shape, split, -0.22, 0.18)
    return jnp.clip(result, -bound, bound).astype(held_as)


def setup_inputs(seed: int = 0) -> dict:
    key_list = jax.random.split(jax.random.key(seed), 13)
    return {
        "traces": normal_values(key_list[0], (NCOMP, NFD, NFACE), 1.0, 6.0, ((0, 4), (2, 128)), jnp.float32),
        "interior_source": normal_values(key_list[1], (NCOMP, NID, ELEMS), 1.0, 6.0, ((0, 4), (2, 128))),
        "orders": draw_orders(jax.random.fold_in(key_list[12], 71), 0),
        "element_scale": jnp.clip(jnp.exp(math.log(2.0) - 1.3862944 * jax.random.uniform(key_list[3], (ELEMS,), jnp.float32) ** block_levels(key_list[3], (ELEMS,), ((0, 128),), -0.2, 0.2)), 0.5, 2.0),
        "element_faces": draw_element_faces(jax.random.fold_in(key_list[12], 71), 0),
        "solver_slots": draw_solver_slots(jax.random.fold_in(key_list[12], 71), 0),
        "line_diagonal": jnp.clip(jnp.exp(math.log(6.0) - 0.87546874 * jax.random.uniform(key_list[6], (NCOMP, NFACE), jnp.float32) ** block_levels(key_list[6], (NCOMP, NFACE), ((0, 4), (1, 128)), -0.2, 0.2)), 2.5, 6.0),
        "species_mix": normal_values(key_list[7], (NCOMP, NCOMP), 0.3, 3.0, ((0, 4),), jnp.float32),
        "couple_in": normal_values(key_list[8], (NCOMP * NID, NCOMP * 4 * NFD), (NCOMP * 4 * NFD) ** -0.5, 0.1875, ((0, 4),)),
        "local_inverse": normal_values(key_list[9], (NCOMP * NID, NCOMP * NID), (NCOMP * NID) ** -0.5, 0.25, ((0, 4),)),
        "trace_block": normal_values(key_list[10], (NCOMP * 4 * NFD, NCOMP * 4 * NFD), (NCOMP * 4 * NFD) ** -0.5, 0.1875, ((0, 4),)),
        "couple_out": normal_values(key_list[11], (NCOMP * 4 * NFD, NCOMP * NID), (NCOMP * NID) ** -0.5, 0.25, ((0, 4),)),
    }


cheb_center = 1.0
cheb_half = 0.8
cheb_ratio = 1.25


def live_masks(orders):
    face_count = (orders + 1) * (orders + 2) // 2
    inner_count = (orders + 1) * (orders + 2) * (orders + 3) // 6
    face_one = jnp.arange(NFD, dtype=jnp.int32)[:, None] < face_count[None, :]
    face_live = jnp.tile(face_one, (4 * NCOMP, 1))
    inner_one = jnp.arange(NID, dtype=jnp.int32)[:, None] < inner_count[None, :]
    inner_live = jnp.tile(inner_one, (NCOMP, 1))
    return face_live, inner_live


def line_apply(values, line_diag):
    padded = jnp.pad(values, ((0, 0), (0, 0), (1, 1)))
    return line_diag * values - (padded[:, :, :-2] + padded[:, :, 2:])


def cheb_sweep(resid, inverse, line_diag):
    step_vec = inverse * resid / cheb_center
    total = step_vec
    rho = 1.0 / cheb_ratio
    for sweep_index in range(DEG - 1):
        rho_next = 1.0 / (2.0 * cheb_ratio - rho)
        step_vec = rho_next * rho * step_vec + (2.0 * rho_next / cheb_half) * inverse * (resid - line_apply(total, line_diag))
        total = total + step_vec
        rho = rho_next
    return total


def wide_dot(left, right):
    return jnp.dot(left.astype(jnp.float32), right.astype(jnp.float32), precision=lax.Precision.HIGHEST)


def reference(traces, interior_source, orders, element_scale, element_faces, solver_slots, line_diagonal, species_mix, couple_in, local_inverse, trace_block, couple_out):
    face_ids = element_faces.reshape(4, N_DOM, E_DEV).transpose(1, 0, 2)
    source_parts = interior_source.reshape(NCOMP * NID, N_DOM, E_DEV).transpose(1, 0, 2)
    order_parts = orders.reshape(N_DOM, E_DEV)
    scale_parts = element_scale.reshape(N_DOM, E_DEV)

    def condense(packed):
        ids, source, part_orders, part_scale = packed
        face_live, inner_live = live_masks(part_orders)
        picked = traces[:, :, ids]
        picked = jnp.transpose(picked, (0, 2, 1, 3)).reshape(NCOMP * 4 * NFD, E_DEV)
        gathered = jnp.where(face_live, picked, 0.0).astype(jnp.bfloat16)
        loads = source.astype(jnp.float32) - wide_dot(couple_in, gathered)
        loads = jnp.where(inner_live, loads, 0.0).astype(jnp.bfloat16)
        interior = jnp.where(inner_live, wide_dot(local_inverse, loads), 0.0).astype(jnp.bfloat16)
        blocks = wide_dot(trace_block, gathered) + wide_dot(couple_out, interior)
        return jnp.where(face_live, blocks, 0.0) * part_scale[None, :]

    block_parts = lax.map(condense, (face_ids, source_parts, order_parts, scale_parts))
    blocks = block_parts.transpose(1, 0, 2).reshape(NCOMP, 4, NFD, ELEMS)
    spread = blocks.transpose(0, 2, 1, 3).reshape(NCOMP, NFD, 4 * ELEMS)
    flat_faces = element_faces.reshape(-1)
    residual = jnp.zeros((NCOMP, NFD, NFACE), jnp.float32).at[:, :, flat_faces].add(spread)
    mixed = residual + jnp.einsum("cd,dkf->ckf", species_mix, residual, precision=lax.Precision.HIGHEST)
    quota = FACE_DEV // N_DOM
    global_slots = (jnp.arange(NFACE, dtype=jnp.int32) // FACE_DEV) * FACE_DEV + solver_slots
    line_rhs = mixed[:, :, global_slots].reshape(NCOMP, NFD, N_DOM, N_DOM, quota).transpose(0, 1, 3, 2, 4).reshape(NCOMP, NFD, NFACE)
    line_diag = line_diagonal[:, None, :]
    inverse = 1.0 / line_diag
    first = cheb_sweep(line_rhs, inverse, line_diag)
    second = cheb_sweep(line_rhs - line_apply(first, line_diag), inverse, line_diag)
    correction = first + second
    sent_back = correction.reshape(NCOMP, NFD, N_DOM, N_DOM, quota).transpose(0, 1, 3, 2, 4).reshape(NCOMP, NFD, NFACE)
    owner_order = jnp.zeros_like(correction).at[:, :, global_slots].set(sent_back)
    return traces - owner_order, mixed
```

```python
import functools

import jax
import jax.numpy as jnp
from jax import lax
from jax.experimental import pallas as pl
from jax.experimental.pallas import tpu as pltpu
from jax.sharding import PartitionSpec as P

F32 = jnp.float32
BF = jnp.bfloat16
I32 = jnp.int32
MESH = pl.DeviceIdType.MESH

NFD = 28
NID = 84
ND = 128
NF = 4
FACES = 512
ELEMS = 256
CK = 64
EXT = 768
RHO0 = 0.8
HALF = 0.8
RATIO = 1.25


def dot(a, b):
    return jnp.dot(a, b, preferred_element_type=F32)


def dot_nt(a, b):
    return lax.dot_general(a, b, (((1,), (1,)), ((), ())), preferred_element_type=F32)


def iota(shape, dim):
    return lax.broadcasted_iota(I32, shape, dim)


def one_hot(cond):
    return jnp.where(cond, 1.0, 0.0).astype(BF)


def hi_lo(x):
    hi = x.astype(BF)
    lo = (x - hi.astype(F32)).astype(BF)
    return jnp.concatenate([hi, lo], axis=0)


def kernel(
    tr_ref, src_ref, ord_ref, scl_ref, fac_ref, slot_ref, dia_ref, mix_ref,
    ci_hbm, li_hbm, tb_hbm, co_hbm,
    new_ref, mixed_ref,
    ta, oh, gat, civ, liv, tbv, cov, cip, lip, tbp, cop, srcf,
    lo_all, in_all, ra, xn, xp, rims, vb, ln, rn, ll, rr,
    s1, r1, r2, r3, dt, dwin, pm, own32, tbg, ownres,
    wsem, ssem, rsem,
):
    d = lax.axis_index("dom")
    f = lax.axis_index("field")
    z = d // 16
    y = (d % 16) // 2
    k = d % 2

    def dom_at(step):
        return (d + step + ND) % ND

    def field_at(step):
        return (f + step) % NF

    loads_w = []
    for i, (src, dst) in enumerate(((ci_hbm, civ), (tb_hbm, tbv), (li_hbm, liv), (co_hbm, cov))):
        c = pltpu.make_async_copy(src, dst, wsem.at[i])
        c.start()
        loads_w.append(c)

    field_peers = [(d, field_at(i)) for i in range(1, NF)]
    next_all = [(dom_at(1), field_at(i)) for i in range(NF)]
    prev_all = [(dom_at(-1), field_at(i)) for i in range(NF)]
    far = [(dom_at(2), f), (dom_at(-2), f)]
    z_peers = [(((z + i) % 8) * 16 + d % 16, f) for i in range(1, 8)]
    y_peers = [(z * 16 + ((y + i) % 8) * 2 + k, f) for i in range(1, 8)]
    core_peer = (d + 1 - 2 * k, f)
    greet = field_peers + next_all + prev_all + far + z_peers + y_peers
    barrier = pltpu.get_barrier_semaphore()
    for dev in greet:
        pl.semaphore_signal(barrier, inc=1, device_id=dev, device_id_type=MESH)

    count = [0]
    sent = []

    def send(src, dst, dev):
        n = count[0]
        count[0] += 1
        c = pltpu.make_async_remote_copy(
            src_ref=src, dst_ref=dst, send_sem=ssem.at[n], recv_sem=rsem.at[n],
            device_id=dev, device_id_type=MESH,
        )
        c.start()
        sent.append(c)
        return c

    pad16 = jnp.zeros((16, ELEMS), BF)
    for g in range(NF):
        lo_all[g, 176:192, :] = pad16
        in_all[g, 176:192, :] = pad16

    own32[...] = jnp.zeros((CK, FACES), F32)
    for c in range(2):
        own32[c * 32 : c * 32 + NFD, :] = tr_ref[:, c, :]
    ta[f, :, 0:FACES] = own32[...].astype(BF)
    dia = jnp.concatenate([dia_ref[...]] * 4, axis=0)
    for zz in range(8):
        s1[zz] = pltpu.roll(dia, (8 - 64 * zz) % FACES, 1)[0:2, 0:128]

    pl.semaphore_wait(barrier, len(greet))

    ex1 = []
    for dev in next_all:
        ex1.append(send(ta.at[f, :, pl.ds(384, 128)], ta.at[f, :, pl.ds(512, 128)], dev))
    for dev in prev_all:
        ex1.append(send(ta.at[f, :, pl.ds(0, 128)], ta.at[f, :, pl.ds(640, 128)], dev))
    for dev in field_peers:
        ex1.append(send(ta.at[f, :, pl.ds(0, FACES)], ta.at[f, :, pl.ds(0, FACES)], dev))
    dz = []
    for i in range(1, 8):
        dz.append(send(s1.at[(z + i) % 8], r1.at[z], z_peers[i - 1]))
    r1[z] = s1[z]

    rel = (fac_ref[...] - d * FACES) & (ND * FACES - 1)
    lid = jnp.where(
        rel < FACES, rel, jnp.where(rel >= ND * FACES - 128, rel - (ND * FACES - 128) + 512, rel + 128)
    )
    for j in range(4):
        oh[:, j * 256 : (j + 1) * 256] = one_hot(iota((EXT, ELEMS), 0) == lid[j : j + 1, :])
    order = ord_ref[...]
    face_n = (order + 1) * (order + 2)
    inner_n = face_n * (order + 3)
    face_live = 2 * (iota((256, ELEMS), 0) & 31) < face_n
    row = iota((2 * NID, ELEMS), 0)
    inner_live = 6 * jnp.where(row >= NID, row - NID, row) < inner_n
    for c in range(2):
        srcf[c * NID : (c + 1) * NID, :] = src_ref[:, c, :].astype(F32)
    zero8 = jnp.zeros((8, ELEMS), F32)

    col = iota((896, 1024), 1)
    kk = col & 31
    want = jnp.where(kk < NFD, ((col >> 5) & 7) * 112 + (col >> 8) * NFD + kk, -1)
    permk = one_hot(iota((896, 1024), 0) == want)
    loads_w[0].wait()
    cip[...] = dot(civ[...], permk).astype(BF)
    rown = iota((256, 224), 0)
    rk = rown & 31
    want_r = jnp.where(rk < NFD, ((rown >> 5) & 1) * 112 + (rown >> 6) * NFD + rk, -1)
    permr = one_hot(iota((256, 224), 1) == want_r)
    loads_w[1].wait()
    tbp[...] = dot(dot(permr, tbv[...]).astype(BF), permk).astype(BF)

    for c in ex1:
        c.wait_recv()
    tall = ta[...].reshape(256, EXT)
    for j in range(4):
        picked = dot(tall, oh[:, j * 256 : (j + 1) * 256])
        gat[j * 256 : (j + 1) * 256, :] = jnp.where(face_live, picked, 0.0).astype(BF)
    loads = srcf[...] - dot(cip[...], gat[...])
    loads = jnp.where(inner_live, loads, 0.0)
    lo_all[f, 0:176] = jnp.concatenate([loads, zero8], axis=0).astype(BF)

    ex2 = [send(lo_all.at[f, pl.ds(0, 176)], lo_all.at[f, pl.ds(0, 176)], dev) for dev in field_peers]
    for c in dz:
        c.wait_recv()
    for c in range(2):
        r2[y, c] = r1[:, c, :]
    dy = []
    for i in range(1, 8):
        dy.append(send(r2.at[y], r2.at[y], y_peers[i - 1]))

    colw = iota((672, EXT), 1)
    slab = (colw >= 192).astype(I32) + (colw >= 384).astype(I32) + (colw >= 576).astype(I32)
    inn = colw - slab * 192
    perms = one_hot(iota((672, EXT), 0) == jnp.where(inn < 168, slab * 168 + inn, -1))
    loads_w[2].wait()
    lip[...] = dot(liv[...], perms).astype(BF)
    loads_w[3].wait()
    cop[...] = dot(dot(permr, cov[...]).astype(BF), perms).astype(BF)
    tbg[...] = dot(tbp[...], gat[...])

    for c in ex2:
        c.wait_recv()
    inter = dot(lip[...], lo_all[...].reshape(EXT, ELEMS))
    inter = jnp.where(inner_live, inter, 0.0)
    in_all[f, 0:176] = jnp.concatenate([inter, zero8], axis=0).astype(BF)

    ex3 = [send(in_all.at[f, pl.ds(0, 176)], in_all.at[f, pl.ds(0, 176)], dev) for dev in field_peers]
    for c in dy:
        c.wait_recv()
    dk = send(r2, r3.at[k], core_peer)
    r3[k] = r2[...]

    slots = slot_ref[...]
    parts = jnp.concatenate([(slots >> 4).astype(F32), (slots & 15).astype(F32)] + [jnp.zeros((6, FACES), F32)], axis=0)
    cs = iota((FACES, FACES), 1)
    spread = one_hot(iota((FACES, FACES), 0) == (cs & 127) * 4 + (cs >> 7))
    moved = dot(parts.astype(BF), spread).astype(I32)
    slot_qt = moved[0:1] * 16 + moved[1:2]
    pm[...] = one_hot(iota((FACES, FACES), 0) == slot_qt)

    for c in ex3:
        c.wait_recv()
    blocks = tbg[...] + dot(cop[...], in_all[...].reshape(EXT, ELEMS))
    blocks = jnp.where(face_live, blocks, 0.0) * scl_ref[...]
    acc = jnp.zeros((2 * CK, EXT), F32)
    for j in range(4):
        acc = acc + dot_nt(hi_lo(blocks[j * CK : (j + 1) * CK]), oh[:, j * 256 : (j + 1) * 256])
    res = acc[0:CK] + acc[CK : 2 * CK]
    ownres[...] = res[:, 0:FACES]
    rims[0] = res[:, 512:640].astype(BF)
    rims[1] = res[:, 640:768].astype(BF)
    ra[f] = res[:, 0:FACES].astype(BF)

    ex4 = []
    for dev in prev_all:
        ex4.append(send(rims.at[0], xn.at[f], dev))
    for dev in next_all:
        ex4.append(send(rims.at[1], xp.at[f], dev))
    for dev in field_peers:
        ex4.append(send(ra.at[f], ra.at[f], dev))

    dk.wait_recv()
    r_i = iota((128, 128), 0)
    t_of = (r_i & 7) * 16 + ((r_i >> 3) & 7) * 2 + (r_i >> 6)
    to_t = one_hot(iota((128, 128), 1) == t_of)
    for c in range(2):
        dt[c] = r3[:, :, c].reshape(128, 128).T
    start = 3 + 4 * (d % 16)
    lane = iota((1, 128), 1)
    for c in range(2):
        win = dt[c, pl.ds(start, 16), :]
        w0 = win.astype(BF)
        rest = win - w0.astype(F32)
        w1 = rest.astype(BF)
        w2 = (rest - w1.astype(F32)).astype(BF)
        got = dot(jnp.concatenate([w0, w1, w2], axis=0), to_t)
        dwin[c] = 1.0 / (got[0:16] + got[16:32] + got[32:48])

    def shifted(v, wrap, step):
        edge = 0 if step == 1 else 127
        rolled = jnp.where(lane == edge, 0.0, pltpu.roll(v, step % 128, 1))
        return jnp.where(wrap, rolled, v)

    wraps = [d <= 1] + [d == 0] * 4 + [None] * 4 + [d == ND - 1] * 4 + [d >= ND - 2]

    def placed(v, i):
        if i < 5:
            return shifted(v, wraps[i], 1)
        if i > 8:
            return shifted(v, wraps[i], -1)
        return v

    inv = []
    for c in range(2):
        inv.append([placed(jnp.broadcast_to(dwin[c, i : i + 1, :], (8, 128)), i) for i in range(14)])

    for c in ex4:
        c.wait_recv()

    mine = ownres[...]
    first_rim = xp[...].astype(F32)
    last_rim = xn[...].astype(F32)
    mixed = [None, None]
    for g in range(NF):
        whole = jnp.where(f == g, mine, ra[g].astype(F32))
        whole = jnp.concatenate(
            [whole[:, 0:128] + first_rim[g], whole[:, 128:384], whole[:, 384:512] + last_rim[g]], axis=1
        )
        for cc in range(2):
            part = whole[cc * 32 : cc * 32 + 32]
            for c in range(2):
                coef = mix_ref[c : c + 1, 2 * g + cc : 2 * g + cc + 1]
                coef = coef + jnp.where((f == g) & (c == cc), 1.0, 0.0)
                term = coef * part
                mixed[c] = term if mixed[c] is None else mixed[c] + term
    both = jnp.concatenate(mixed, axis=0)
    moved_rhs = dot(hi_lo(both), pm[...])
    rhs = moved_rhs[0:CK] + moved_rhs[CK : 2 * CK]
    vb[...] = rhs.astype(BF)

    ex5 = [
        send(vb, ln, (dom_at(1), f)),
        send(vb, rn, (dom_at(-1), f)),
        send(vb.at[:, pl.ds(384, 128)], ll, far[0]),
        send(vb.at[:, pl.ds(0, 128)], rr, far[1]),
    ]
    for c in range(2):
        mixed_ref[c] = mixed[c][0:NFD]
    for c in ex5:
        c.wait_recv()

    corr = []
    for b in range(8):
        rows = slice(b * 8, b * 8 + 8)
        iv = inv[b // 4]
        pair = slice((b // 2) * 16, (b // 2) * 16 + 16)
        half = slice((b % 2) * 8, (b % 2) * 8 + 8)

        def get(ref, q):
            return ref[pair, q * 128 : (q + 1) * 128].astype(F32)[half]

        r = [get(ll, 0)] + [get(ln, q) for q in range(4)] + [rhs[rows, q * 128 : (q + 1) * 128] for q in range(4)]
        r = r + [get(rn, q) for q in range(4)] + [get(rr, 0)]
        yv = {i: iv[i] * placed(r[i], i) for i in range(14)}

        def residual(yy, zz, lo, hi):
            return {i: yy[i] + iv[i] * (zz[i - 1] + zz[i + 1]) - zz[i] for i in range(lo, hi)}

        def sweep(yy, lo, hi):
            step = dict(yy)
            total = dict(yy)
            rho = RHO0
            for _ in range(2):
                lo, hi = lo + 1, hi - 1
                rho_next = 1.0 / (2.0 * RATIO - rho)
                u = residual(yy, total, lo, hi)
                step = {i: (rho_next * rho) * step[i] + (2.0 * rho_next / HALF) * u[i] for i in range(lo, hi)}
                total = {i: total[i] + step[i] for i in range(lo, hi)}
                rho = rho_next
            return total, lo, hi

        first, lo, hi = sweep(yv, 0, 14)
        y2 = residual(yv, first, lo + 1, hi - 1)
        second, lo, hi = sweep(y2, lo + 1, hi - 1)
        corr.append(jnp.concatenate([first[i] + second[i] for i in range(5, 9)], axis=1))
    corr = jnp.concatenate(corr, axis=0)
    back = dot_nt(hi_lo(corr), pm[...])
    new = own32[...] - (back[0:CK] + back[CK : 2 * CK])
    for c in range(2):
        new_ref[c] = new[c * 32 : c * 32 + NFD]
    for c in sent:
        c.wait_send()


def shards(
    traces,
    interior_source,
    orders,
    element_scale,
    element_faces,
    solver_slots,
    line_diagonal,
    species_mix,
    couple_in,
    local_inverse,
    trace_block,
    couple_out,
):
    vmem = pl.BlockSpec(memory_space=pltpu.VMEM)
    anyw = pl.BlockSpec(memory_space=pl.ANY)
    n_copies = 64
    scratch = [
        pltpu.VMEM((NF, CK, EXT), BF),
        pltpu.VMEM((EXT, 1024), BF),
        pltpu.VMEM((1024, ELEMS), BF),
        pltpu.VMEM((168, 896), BF),
        pltpu.VMEM((168, 672), BF),
        pltpu.VMEM((224, 896), BF),
        pltpu.VMEM((224, 672), BF),
        pltpu.VMEM((168, 1024), BF),
        pltpu.VMEM((168, EXT), BF),
        pltpu.VMEM((256, 1024), BF),
        pltpu.VMEM((256, EXT), BF),
        pltpu.VMEM((168, ELEMS), F32),
        pltpu.VMEM((NF, 192, ELEMS), BF),
        pltpu.VMEM((NF, 192, ELEMS), BF),
        pltpu.VMEM((NF, CK, FACES), BF),
        pltpu.VMEM((NF, CK, 128), BF),
        pltpu.VMEM((NF, CK, 128), BF),
        pltpu.VMEM((2, CK, 128), BF),
        pltpu.VMEM((CK, FACES), BF),
        pltpu.VMEM((CK, FACES), BF),
        pltpu.VMEM((CK, FACES), BF),
        pltpu.VMEM((CK, 128), BF),
        pltpu.VMEM((CK, 128), BF),
        pltpu.VMEM((8, 2, 128), F32),
        pltpu.VMEM((8, 2, 128), F32),
        pltpu.VMEM((8, 2, 8, 128), F32),
        pltpu.VMEM((2, 8, 2, 8, 128), F32),
        pltpu.VMEM((2, 128, 128), F32),
        pltpu.VMEM((2, 16, 128), F32),
        pltpu.VMEM((FACES, FACES), BF),
        pltpu.VMEM((CK, FACES), F32),
        pltpu.VMEM((256, ELEMS), F32),
        pltpu.VMEM((CK, FACES), F32),
        pltpu.SemaphoreType.DMA((4,)),
        pltpu.SemaphoreType.DMA((n_copies,)),
        pltpu.SemaphoreType.DMA((n_copies,)),
    ]
    shape = jax.ShapeDtypeStruct((2, NFD, FACES), F32)
    new, mixed = pl.pallas_call(
        kernel,
        out_shape=(shape, shape),
        in_specs=[vmem] * 8 + [anyw] * 4,
        out_specs=(vmem, vmem),
        scratch_shapes=scratch,
        compiler_params=pltpu.CompilerParams(
            collective_id=0, has_side_effects=True, vmem_limit_bytes=48 * 1024 * 1024
        ),
    )(
        jnp.transpose(traces, (1, 0, 2)),
        jnp.transpose(interior_source, (1, 0, 2)),
        orders.reshape(1, ELEMS),
        element_scale.reshape(1, ELEMS),
        element_faces,
        solver_slots.reshape(1, FACES),
        line_diagonal,
        species_mix,
        couple_in,
        local_inverse,
        trace_block,
        couple_out,
    )
    return new, mixed


def solution(mesh):
    in_specs = (
        P("field", None, "dom"),
        P("field", None, "dom"),
        P("dom"),
        P("dom"),
        P(None, "dom"),
        P("dom"),
        P("field", "dom"),
        P("field", None),
        P("field", None),
        P("field", None),
        P("field", None),
        P("field", None),
    )
    out_specs = (P("field", None, "dom"), P("field", None, "dom"))
    return jax.shard_map(shards, mesh=mesh, in_specs=in_specs, out_specs=out_specs, check_vma=False)
```

```python
import functools

import jax
import jax.numpy as jnp
from jax import lax
from jax.experimental import pallas as pl
from jax.experimental.pallas import tpu as pltpu
from jax.sharding import PartitionSpec as P

F32 = jnp.float32
BF = jnp.bfloat16
I32 = jnp.int32
MESH = pl.DeviceIdType.MESH

NFD = 28
NID = 84
ND = 128
NF = 4
FACES = 512
ELEMS = 256
CK = 64
EXT = 640
PADK = 768
HE = 128
RIM = 32
RHO0 = 0.8
HALF = 0.8
RATIO = 1.25


def dot(a, b):
    return jnp.dot(a, b, preferred_element_type=F32)


def dot_nt(a, b):
    return lax.dot_general(a, b, (((1,), (1,)), ((), ())), preferred_element_type=F32)


def iota(shape, dim):
    return lax.broadcasted_iota(I32, shape, dim)


def one_hot(cond):
    return jnp.where(cond, 1.0, 0.0).astype(BF)


def hi_lo(x):
    hi = x.astype(BF)
    lo = (x - hi.astype(F32)).astype(BF)
    return jnp.concatenate([hi, lo], axis=0)


def packed_rim(x, lane0):
    lane = iota((16, 128), 1)
    out = jnp.zeros((16, 128), F32)
    for i in range(4):
        part = pltpu.roll(x[16 * i : 16 * i + 16], (RIM * i - lane0) % 128, 1)
        out = jnp.where((lane >= RIM * i) & (lane < RIM * i + RIM), part, out)
    return out


def unpacked_rim(x, lane0):
    lane = iota((16, 128), 1)
    keep = (lane >= lane0) & (lane < lane0 + RIM)
    parts = [jnp.where(keep, pltpu.roll(x, (lane0 - RIM * i) % 128, 1), 0.0) for i in range(4)]
    return jnp.concatenate(parts, axis=0)


def kernel(
    dia_hbm, tr_hbm, fac_hbm, ord_hbm, src_hbm, ci_hbm, tb_hbm, li_hbm, co_hbm, slot_hbm, scl_hbm, mix_hbm,
    new_ref, mixed_ref,
    ta, oh, gat, civ, liv, tbv, cov, cip, lip, tbp, cop, srcf,
    lo_all, in_all, ra, rim1, xr1, rim4, xr4, vb, ln, rn, ll, rr,
    s1, r1, r2, r3, dt, dwin, pm, own32, tbg, ownres,
    dia_ref, tr_ref, fac_ref, ord_ref, src_ref, slot_ref, scl_ref, mix_ref,
    wsem, ssem, rsem,
):
    d = lax.axis_index("dom")
    f = lax.axis_index("field")
    z = d // 16
    y = (d % 16) // 2
    k = d % 2

    def dom_at(step):
        return (d + step + ND) % ND

    def field_at(step):
        return (f + step) % NF

    pairs = (
        (dia_hbm, dia_ref), (tr_hbm, tr_ref), (fac_hbm, fac_ref), (ord_hbm, ord_ref), (src_hbm, src_ref),
        (ci_hbm, civ), (tb_hbm, tbv), (li_hbm, liv), (co_hbm, cov),
        (slot_hbm, slot_ref), (scl_hbm, scl_ref), (mix_hbm, mix_ref),
    )
    fetch = [pltpu.make_async_copy(src, dst, wsem.at[i]) for i, (src, dst) in enumerate(pairs)]
    for c in fetch:
        c.start()

    field_peers = [(d, field_at(i)) for i in range(1, NF)]
    next_all = [(dom_at(1), field_at(i)) for i in range(NF)]
    prev_all = [(dom_at(-1), field_at(i)) for i in range(NF)]
    far = [(dom_at(2), f), (dom_at(-2), f)]
    z_peers = [(((z + i) % 8) * 16 + d % 16, f) for i in range(1, 8)]
    y_peers = [(z * 16 + ((y + i) % 8) * 2 + k, f) for i in range(1, 8)]
    core_peer = (d + 1 - 2 * k, f)
    greet = field_peers + next_all + prev_all + far + z_peers + y_peers
    barrier = pltpu.get_barrier_semaphore()
    for dev in greet:
        pl.semaphore_signal(barrier, inc=1, device_id=dev, device_id_type=MESH)

    count = [0]
    sent = []

    def send(src, dst, dev):
        n = count[0]
        count[0] += 1
        c = pltpu.make_async_remote_copy(
            src_ref=src, dst_ref=dst, send_sem=ssem.at[n], recv_sem=rsem.at[n],
            device_id=dev, device_id_type=MESH,
        )
        c.start()
        sent.append(c)
        return c

    pad16 = jnp.zeros((16, HE), BF)
    for g in range(NF):
        for h in range(2):
            lo_all[h, g, 176:192, :] = pad16
            in_all[h, g, 176:192, :] = pad16

    own32[...] = jnp.zeros((CK, FACES), F32)
    fetch[1].wait()
    for c in range(2):
        own32[c * 32 : c * 32 + NFD, :] = tr_ref[:, c, :]
    ta[f, :, 0:FACES] = own32[...].astype(BF)
    rim1[0] = packed_rim(own32[:, 0:128], 0).astype(BF)
    rim1[1] = packed_rim(own32[:, 384:512], 96).astype(BF)
    fetch[0].wait()
    dia = jnp.concatenate([dia_ref[...]] * 4, axis=0)
    for zz in range(8):
        s1[zz] = pltpu.roll(dia, (8 - 64 * zz) % FACES, 1)[0:2, 0:128]

    pl.semaphore_wait(barrier, len(greet))

    ex1 = []
    for dev in next_all:
        ex1.append(send(rim1.at[1], xr1.at[0, f], dev))
    for dev in prev_all:
        ex1.append(send(rim1.at[0], xr1.at[1, f], dev))
    for dev in field_peers:
        ex1.append(send(ta.at[f, :, pl.ds(0, FACES)], ta.at[f, :, pl.ds(0, FACES)], dev))
    dz = []
    for i in range(1, 8):
        dz.append(send(s1.at[(z + i) % 8], r1.at[z], z_peers[i - 1]))
    r1[z] = s1[z]

    fetch[2].wait()
    rel = (fac_ref[...] - d * FACES) & (ND * FACES - 1)
    lid = jnp.where(
        rel < FACES, rel, jnp.where(rel >= ND * FACES - RIM, rel - (ND * FACES - RIM) + FACES, rel + RIM)
    )
    for h in range(2):
        for j in range(4):
            c0 = h * 512 + j * HE
            oh[:, c0 : c0 + HE] = one_hot(iota((EXT, HE), 0) == lid[j : j + 1, h * HE : h * HE + HE])
    fetch[3].wait()
    order = ord_ref[...]
    face_n = (order + 1) * (order + 2)
    inner_n = face_n * (order + 3)
    face_live = 2 * (iota((256, ELEMS), 0) & 31) < face_n
    row = iota((2 * NID, ELEMS), 0)
    inner_live = 6 * jnp.where(row >= NID, row - NID, row) < inner_n
    fetch[4].wait()
    for c in range(2):
        srcf[c * NID : (c + 1) * NID, :] = src_ref[:, c, :].astype(F32)
    zero8 = jnp.zeros((8, HE), F32)

    col = iota((896, 1024), 1)
    kk = col & 31
    want = jnp.where(kk < NFD, ((col >> 5) & 7) * 112 + (col >> 8) * NFD + kk, -1)
    permk = one_hot(iota((896, 1024), 0) == want)
    fetch[5].wait()
    cip[...] = dot(civ[...], permk).astype(BF)
    rown = iota((256, 224), 0)
    rk = rown & 31
    want_r = jnp.where(rk < NFD, ((rown >> 5) & 1) * 112 + (rown >> 6) * NFD + rk, -1)
    permr = one_hot(iota((256, 224), 1) == want_r)
    fetch[6].wait()
    tbp[...] = dot(dot(permr, tbv[...]).astype(BF), permk).astype(BF)

    for c in ex1:
        c.wait_recv()
    for g in range(NF):
        ta[g, :, FACES:EXT] = (
            unpacked_rim(xr1[0, g].astype(F32), 0) + unpacked_rim(xr1[1, g].astype(F32), RIM)
        ).astype(BF)
    tall = ta[...].reshape(256, EXT)
    ex2 = [[], []]
    for h in range(2):
        es = slice(h * HE, h * HE + HE)
        picked = dot(tall, oh[:, h * 512 : h * 512 + 512])
        for j in range(4):
            live = jnp.where(face_live[:, es], picked[:, j * HE : (j + 1) * HE], 0.0)
            gat[h, j * 256 : (j + 1) * 256, :] = live.astype(BF)
        loads = srcf[:, es] - dot(cip[...], gat[h])
        loads = jnp.where(inner_live[:, es], loads, 0.0)
        lo_all[h, f, 0:176] = jnp.concatenate([loads, zero8], axis=0).astype(BF)
        for dev in field_peers:
            ex2[h].append(send(lo_all.at[h, f, pl.ds(0, 176)], lo_all.at[h, f, pl.ds(0, 176)], dev))
    for c in dz:
        c.wait_recv()
    for c in range(2):
        r2[y, c] = r1[:, c, :]
    dy = []
    for i in range(1, 8):
        dy.append(send(r2.at[y], r2.at[y], y_peers[i - 1]))

    colw = iota((672, PADK), 1)
    slab = (colw >= 192).astype(I32) + (colw >= 384).astype(I32) + (colw >= 576).astype(I32)
    inn = colw - slab * 192
    perms = one_hot(iota((672, PADK), 0) == jnp.where(inn < 168, slab * 168 + inn, -1))
    fetch[7].wait()
    lip[...] = dot(liv[...], perms).astype(BF)
    fetch[8].wait()
    cop[...] = dot(dot(permr, cov[...]).astype(BF), perms).astype(BF)
    for h in range(2):
        tbg[h] = dot(tbp[...], gat[h])

    ex3 = [[], []]
    for h in range(2):
        es = slice(h * HE, h * HE + HE)
        for c in ex2[h]:
            c.wait_recv()
        inter = dot(lip[...], lo_all[h].reshape(PADK, HE))
        inter = jnp.where(inner_live[:, es], inter, 0.0)
        in_all[h, f, 0:176] = jnp.concatenate([inter, zero8], axis=0).astype(BF)
        for dev in field_peers:
            ex3[h].append(send(in_all.at[h, f, pl.ds(0, 176)], in_all.at[h, f, pl.ds(0, 176)], dev))
    for c in dy:
        c.wait_recv()
    dk = send(r2, r3.at[k], core_peer)
    r3[k] = r2[...]

    fetch[9].wait()
    slots = slot_ref[...]
    parts = jnp.concatenate([(slots >> 4).astype(F32), (slots & 15).astype(F32)] + [jnp.zeros((6, FACES), F32)], axis=0)
    cs = iota((FACES, FACES), 1)
    spread = one_hot(iota((FACES, FACES), 0) == (cs & 127) * 4 + (cs >> 7))
    moved = dot(parts.astype(BF), spread).astype(I32)
    slot_qt = moved[0:1] * 16 + moved[1:2]
    pm[...] = one_hot(iota((FACES, FACES), 0) == slot_qt)

    fetch[10].wait()
    fetch[11].wait()
    acc = jnp.zeros((2 * CK, EXT), F32)
    for h in range(2):
        es = slice(h * HE, h * HE + HE)
        for c in ex3[h]:
            c.wait_recv()
        blocks = tbg[h] + dot(cop[...], in_all[h].reshape(PADK, HE))
        blocks = jnp.where(face_live[:, es], blocks, 0.0) * scl_ref[:, es]
        wide = jnp.concatenate([blocks[j * CK : (j + 1) * CK] for j in range(4)], axis=1)
        acc = acc + dot_nt(hi_lo(wide), oh[:, h * 512 : h * 512 + 512])
    res = acc[0:CK] + acc[CK : 2 * CK]
    ownres[...] = res[:, 0:FACES]
    rim4[0] = packed_rim(res[:, FACES:EXT], 0).astype(BF)
    rim4[1] = packed_rim(res[:, FACES:EXT], RIM).astype(BF)
    ra[f] = res[:, 0:FACES].astype(BF)

    ex4 = []
    for dev in prev_all:
        ex4.append(send(rim4.at[0], xr4.at[0, f], dev))
    for dev in next_all:
        ex4.append(send(rim4.at[1], xr4.at[1, f], dev))
    for dev in field_peers:
        ex4.append(send(ra.at[f], ra.at[f], dev))

    dk.wait_recv()
    r_i = iota((128, 128), 0)
    t_of = (r_i & 7) * 16 + ((r_i >> 3) & 7) * 2 + (r_i >> 6)
    to_t = one_hot(iota((128, 128), 1) == t_of)
    for c in range(2):
        dt[c] = r3[:, :, c].reshape(128, 128).T
    start = 3 + 4 * (d % 16)
    lane = iota((1, 128), 1)
    for c in range(2):
        win = dt[c, pl.ds(start, 16), :]
        w0 = win.astype(BF)
        rest = win - w0.astype(F32)
        w1 = rest.astype(BF)
        w2 = (rest - w1.astype(F32)).astype(BF)
        got = dot(jnp.concatenate([w0, w1, w2], axis=0), to_t)
        dwin[c] = 1.0 / (got[0:16] + got[16:32] + got[32:48])

    def shifted(v, wrap, step):
        edge = 0 if step == 1 else 127
        rolled = jnp.where(lane == edge, 0.0, pltpu.roll(v, step % 128, 1))
        return jnp.where(wrap, rolled, v)

    wraps = [d <= 1] + [d == 0] * 4 + [None] * 4 + [d == ND - 1] * 4 + [d >= ND - 2]

    def placed(v, i):
        if i < 5:
            return shifted(v, wraps[i], 1)
        if i > 8:
            return shifted(v, wraps[i], -1)
        return v

    inv = []
    for c in range(2):
        inv.append([placed(jnp.broadcast_to(dwin[c, i : i + 1, :], (8, 128)), i) for i in range(14)])

    for c in ex4:
        c.wait_recv()

    mine = ownres[...]
    mixed = [None, None]
    for g in range(NF):
        whole = jnp.where(f == g, mine, ra[g].astype(F32))
        whole = jnp.concatenate(
            [
                whole[:, 0:128] + unpacked_rim(xr4[1, g].astype(F32), 0),
                whole[:, 128:384],
                whole[:, 384:512] + unpacked_rim(xr4[0, g].astype(F32), 96),
            ],
            axis=1,
        )
        for cc in range(2):
            part = whole[cc * 32 : cc * 32 + 32]
            for c in range(2):
                coef = mix_ref[c : c + 1, 2 * g + cc : 2 * g + cc + 1]
                coef = coef + jnp.where((f == g) & (c == cc), 1.0, 0.0)
                term = coef * part
                mixed[c] = term if mixed[c] is None else mixed[c] + term
    both = jnp.concatenate(mixed, axis=0)
    moved_rhs = dot(hi_lo(both), pm[...])
    rhs = moved_rhs[0:CK] + moved_rhs[CK : 2 * CK]
    vb[...] = rhs.astype(BF)

    ex5 = [
        send(vb, ln, (dom_at(1), f)),
        send(vb, rn, (dom_at(-1), f)),
        send(vb.at[:, pl.ds(384, 128)], ll, far[0]),
        send(vb.at[:, pl.ds(0, 128)], rr, far[1]),
    ]
    for c in range(2):
        mixed_ref[c] = mixed[c][0:NFD]
    for c in ex5:
        c.wait_recv()

    corr = []
    for b in range(8):
        rows = slice(b * 8, b * 8 + 8)
        iv = inv[b // 4]
        pair = slice((b // 2) * 16, (b // 2) * 16 + 16)
        half = slice((b % 2) * 8, (b % 2) * 8 + 8)

        def get(ref, q):
            return ref[pair, q * 128 : (q + 1) * 128].astype(F32)[half]

        r = [get(ll, 0)] + [get(ln, q) for q in range(4)] + [rhs[rows, q * 128 : (q + 1) * 128] for q in range(4)]
        r = r + [get(rn, q) for q in range(4)] + [get(rr, 0)]
        yv = {i: iv[i] * placed(r[i], i) for i in range(14)}

        def residual(yy, zz, lo, hi):
            return {i: yy[i] + iv[i] * (zz[i - 1] + zz[i + 1]) - zz[i] for i in range(lo, hi)}

        def sweep(yy, lo, hi):
            step = dict(yy)
            total = dict(yy)
            rho = RHO0
            for _ in range(2):
                lo, hi = lo + 1, hi - 1
                rho_next = 1.0 / (2.0 * RATIO - rho)
                u = residual(yy, total, lo, hi)
                step = {i: (rho_next * rho) * step[i] + (2.0 * rho_next / HALF) * u[i] for i in range(lo, hi)}
                total = {i: total[i] + step[i] for i in range(lo, hi)}
                rho = rho_next
            return total, lo, hi

        first, lo, hi = sweep(yv, 0, 14)
        y2 = residual(yv, first, lo + 1, hi - 1)
        second, lo, hi = sweep(y2, lo + 1, hi - 1)
        corr.append(jnp.concatenate([first[i] + second[i] for i in range(5, 9)], axis=1))
    corr = jnp.concatenate(corr, axis=0)
    back = dot_nt(hi_lo(corr), pm[...])
    new = own32[...] - (back[0:CK] + back[CK : 2 * CK])
    for c in range(2):
        new_ref[c] = new[c * 32 : c * 32 + NFD]
    for c in sent:
        c.wait_send()


def shards(
    traces,
    interior_source,
    orders,
    element_scale,
    element_faces,
    solver_slots,
    line_diagonal,
    species_mix,
    couple_in,
    local_inverse,
    trace_block,
    couple_out,
):
    vmem = pl.BlockSpec(memory_space=pltpu.VMEM)
    hbm = pl.BlockSpec(memory_space=pltpu.HBM)
    n_copies = 64
    scratch = [
        pltpu.VMEM((NF, CK, EXT), BF),
        pltpu.VMEM((EXT, 1024), BF),
        pltpu.VMEM((2, 1024, HE), BF),
        pltpu.VMEM((168, 896), BF),
        pltpu.VMEM((168, 672), BF),
        pltpu.VMEM((224, 896), BF),
        pltpu.VMEM((224, 672), BF),
        pltpu.VMEM((168, 1024), BF),
        pltpu.VMEM((168, PADK), BF),
        pltpu.VMEM((256, 1024), BF),
        pltpu.VMEM((256, PADK), BF),
        pltpu.VMEM((168, ELEMS), F32),
        pltpu.VMEM((2, NF, 192, HE), BF),
        pltpu.VMEM((2, NF, 192, HE), BF),
        pltpu.VMEM((NF, CK, FACES), BF),
        pltpu.VMEM((2, 16, 128), BF),
        pltpu.VMEM((2, NF, 16, 128), BF),
        pltpu.VMEM((2, 16, 128), BF),
        pltpu.VMEM((2, NF, 16, 128), BF),
        pltpu.VMEM((CK, FACES), BF),
        pltpu.VMEM((CK, FACES), BF),
        pltpu.VMEM((CK, FACES), BF),
        pltpu.VMEM((CK, 128), BF),
        pltpu.VMEM((CK, 128), BF),
        pltpu.VMEM((8, 2, 128), F32),
        pltpu.VMEM((8, 2, 128), F32),
        pltpu.VMEM((8, 2, 8, 128), F32),
        pltpu.VMEM((2, 8, 2, 8, 128), F32),
        pltpu.VMEM((2, 128, 128), F32),
        pltpu.VMEM((2, 16, 128), F32),
        pltpu.VMEM((FACES, FACES), BF),
        pltpu.VMEM((CK, FACES), F32),
        pltpu.VMEM((2, 256, HE), F32),
        pltpu.VMEM((CK, FACES), F32),
        pltpu.VMEM((2, FACES), F32),
        pltpu.VMEM((NFD, 2, FACES), F32),
        pltpu.VMEM((4, ELEMS), I32),
        pltpu.VMEM((1, ELEMS), I32),
        pltpu.VMEM((NID, 2, ELEMS), BF),
        pltpu.VMEM((1, FACES), I32),
        pltpu.VMEM((1, ELEMS), F32),
        pltpu.VMEM((2, 8), F32),
        pltpu.SemaphoreType.DMA((12,)),
        pltpu.SemaphoreType.DMA((n_copies,)),
        pltpu.SemaphoreType.DMA((n_copies,)),
    ]
    shape = jax.ShapeDtypeStruct((2, NFD, FACES), F32)
    new, mixed = pl.pallas_call(
        kernel,
        out_shape=(shape, shape),
        in_specs=[hbm] * 12,
        out_specs=(vmem, vmem),
        scratch_shapes=scratch,
        compiler_params=pltpu.CompilerParams(
            collective_id=0, has_side_effects=True, vmem_limit_bytes=62 * 1024 * 1024
        ),
    )(
        line_diagonal,
        jnp.transpose(traces, (1, 0, 2)),
        element_faces,
        orders.reshape(1, ELEMS),
        jnp.transpose(interior_source, (1, 0, 2)),
        couple_in,
        trace_block,
        local_inverse,
        couple_out,
        solver_slots.reshape(1, FACES),
        element_scale.reshape(1, ELEMS),
        species_mix,
    )
    return new, mixed


def solution(mesh):
    in_specs = (
        P("field", None, "dom"),
        P("field", None, "dom"),
        P("dom"),
        P("dom"),
        P(None, "dom"),
        P("dom"),
        P("field", "dom"),
        P("field", None),
        P("field", None),
        P("field", None),
        P("field", None),
        P("field", None),
    )
    out_specs = (P("field", None, "dom"), P("field", None, "dom"))
    return jax.shard_map(shards, mesh=mesh, in_specs=in_specs, out_specs=out_specs, check_vma=False)
```

```python
import functools

import jax
import jax.numpy as jnp
from jax import lax
from jax.experimental import pallas as pl
from jax.experimental.pallas import tpu as pltpu
from jax.sharding import PartitionSpec as P

F32 = jnp.float32
BF = jnp.bfloat16
I32 = jnp.int32
MESH = pl.DeviceIdType.MESH

NFD = 28
NID = 84
ND = 128
NF = 4
FACES = 512
ELEMS = 256
CK = 64
EXT = 640
PADK = 768
HE = 128
RIM = 32
RHO0 = 0.8
HALF = 0.8
RATIO = 1.25


def dot(a, b):
    return jnp.dot(a, b, preferred_element_type=F32)


def dot_nt(a, b):
    return lax.dot_general(a, b, (((1,), (1,)), ((), ())), preferred_element_type=F32)


def iota(shape, dim):
    return lax.broadcasted_iota(I32, shape, dim)


def one_hot(cond):
    return jnp.where(cond, 1.0, 0.0).astype(BF)


def hi_lo(x):
    hi = x.astype(BF)
    lo = (x - hi.astype(F32)).astype(BF)
    return jnp.concatenate([hi, lo], axis=0)


def packed_rim(x, lane0):
    lane = iota((16, 128), 1)
    out = jnp.zeros((16, 128), F32)
    for i in range(4):
        part = pltpu.roll(x[16 * i : 16 * i + 16], (RIM * i - lane0) % 128, 1)
        out = jnp.where((lane >= RIM * i) & (lane < RIM * i + RIM), part, out)
    return out


def unpacked_rim(x, lane0):
    lane = iota((16, 128), 1)
    keep = (lane >= lane0) & (lane < lane0 + RIM)
    parts = [jnp.where(keep, pltpu.roll(x, (lane0 - RIM * i) % 128, 1), 0.0) for i in range(4)]
    return jnp.concatenate(parts, axis=0)


def kernel(
    dia_hbm, tr_hbm, fac_hbm, ord_hbm, src_hbm, ci_hbm, tb_hbm, li_hbm, co_hbm, slot_hbm, scl_hbm, mix_hbm,
    new_ref, mixed_ref,
    ta, oh, gat, civ, liv, tbv, cov, cip, lip, tbp, cop, srcf,
    lo_all, in_all, ra, rim1, xr1, rim4, xr4, vb, ln, rn, ll, rr,
    s1, r1, r2, r3, dt, dwin, pm, own32, tbg, ownres,
    dia_ref, tr_ref, fac_ref, ord_ref, src_ref, slot_ref, scl_ref, mix_ref,
    wsem, ssem, rsem,
):
    d = lax.axis_index("dom")
    f = lax.axis_index("field")
    z = d // 16
    y = (d % 16) // 2
    k = d % 2

    def dom_at(step):
        return (d + step + ND) % ND

    def field_at(step):
        return (f + step) % NF

    pairs = (
        (dia_hbm, dia_ref), (tr_hbm, tr_ref), (fac_hbm, fac_ref), (ord_hbm, ord_ref), (src_hbm, src_ref),
        (ci_hbm, civ), (tb_hbm, tbv), (li_hbm, liv), (co_hbm, cov),
        (slot_hbm, slot_ref), (scl_hbm, scl_ref), (mix_hbm, mix_ref),
    )
    fetch = [pltpu.make_async_copy(src, dst, wsem.at[i]) for i, (src, dst) in enumerate(pairs)]
    for c in fetch:
        c.start()

    field_peers = [(d, field_at(i)) for i in range(1, NF)]
    next_all = [(dom_at(1), field_at(i)) for i in range(NF)]
    prev_all = [(dom_at(-1), field_at(i)) for i in range(NF)]
    far = [(dom_at(2), f), (dom_at(-2), f)]
    z_peers = [(((z + i) % 8) * 16 + d % 16, f) for i in range(1, 8)]
    y_peers = [(z * 16 + ((y + i) % 8) * 2 + k, f) for i in range(1, 8)]
    core_peer = (d + 1 - 2 * k, f)
    greet = field_peers + next_all + prev_all + far + z_peers + y_peers
    barrier = pltpu.get_barrier_semaphore()
    for dev in greet:
        pl.semaphore_signal(barrier, inc=1, device_id=dev, device_id_type=MESH)

    count = [0]
    sent = []

    def send(src, dst, dev):
        n = count[0]
        count[0] += 1
        c = pltpu.make_async_remote_copy(
            src_ref=src, dst_ref=dst, send_sem=ssem.at[n], recv_sem=rsem.at[n],
            device_id=dev, device_id_type=MESH,
        )
        c.start()
        sent.append(c)
        return c

    pad16 = jnp.zeros((16, HE), BF)
    for g in range(NF):
        for h in range(2):
            lo_all[h, g, 176:192, :] = pad16
            in_all[h, g, 176:192, :] = pad16

    own32[...] = jnp.zeros((CK, FACES), F32)
    fetch[1].wait()
    for c in range(2):
        own32[c * 32 : c * 32 + NFD, :] = tr_ref[:, c, :]
    ta[f, :, 0:FACES] = own32[...].astype(BF)
    rim1[0] = packed_rim(own32[:, 0:128], 0).astype(BF)
    rim1[1] = packed_rim(own32[:, 384:512], 96).astype(BF)
    fetch[0].wait()
    dia = jnp.concatenate([dia_ref[...]] * 4, axis=0)
    for zz in range(8):
        s1[zz] = pltpu.roll(dia, (8 - 64 * zz) % FACES, 1)[0:2, 0:128]

    pl.semaphore_wait(barrier, len(greet))

    ex1 = []
    for dev in next_all:
        ex1.append(send(rim1.at[1], xr1.at[0, f], dev))
    for dev in prev_all:
        ex1.append(send(rim1.at[0], xr1.at[1, f], dev))
    for dev in field_peers:
        ex1.append(send(ta.at[f, :, pl.ds(0, FACES)], ta.at[f, :, pl.ds(0, FACES)], dev))
    dz = []
    for i in range(1, 8):
        dz.append(send(s1.at[(z + i) % 8], r1.at[z], z_peers[i - 1]))
    r1[z] = s1[z]

    fetch[2].wait()
    rel = (fac_ref[...] - d * FACES) & (ND * FACES - 1)
    lid = jnp.where(
        rel < FACES, rel, jnp.where(rel >= ND * FACES - RIM, rel - (ND * FACES - RIM) + FACES, rel + RIM)
    )
    for h in range(2):
        for j in range(4):
            c0 = h * 512 + j * HE
            oh[:, c0 : c0 + HE] = one_hot(iota((EXT, HE), 0) == lid[j : j + 1, h * HE : h * HE + HE])
    fetch[3].wait()
    order = ord_ref[...]
    face_n = (order + 1) * (order + 2)
    inner_n = face_n * (order + 3)
    face_live = 2 * (iota((256, ELEMS), 0) & 31) < face_n
    row = iota((2 * NID, ELEMS), 0)
    inner_live = 6 * jnp.where(row >= NID, row - NID, row) < inner_n
    fetch[4].wait()
    for c in range(2):
        srcf[c * NID : (c + 1) * NID, :] = src_ref[:, c, :].astype(F32)
    zero8 = jnp.zeros((8, HE), F32)

    col = iota((896, 1024), 1)
    kk = col & 31
    want = jnp.where(kk < NFD, ((col >> 5) & 7) * 112 + (col >> 8) * NFD + kk, -1)
    permk = one_hot(iota((896, 1024), 0) == want)
    fetch[5].wait()
    cip[...] = dot(civ[...], permk).astype(BF)
    rown = iota((256, 224), 0)
    rk = rown & 31
    want_r = jnp.where(rk < NFD, ((rown >> 5) & 1) * 112 + (rown >> 6) * NFD + rk, -1)
    permr = one_hot(iota((256, 224), 1) == want_r)
    fetch[6].wait()
    tbp[...] = dot(dot(permr, tbv[...]).astype(BF), permk).astype(BF)

    for c in ex1:
        c.wait_recv()
    for g in range(NF):
        ta[g, :, FACES:EXT] = (
            unpacked_rim(xr1[0, g].astype(F32), 0) + unpacked_rim(xr1[1, g].astype(F32), RIM)
        ).astype(BF)
    tall = ta[...].reshape(256, EXT)
    ex2 = [[], []]
    for h in range(2):
        es = slice(h * HE, h * HE + HE)
        picked = dot(tall, oh[:, h * 512 : h * 512 + 512])
        for j in range(4):
            live = jnp.where(face_live[:, es], picked[:, j * HE : (j + 1) * HE], 0.0)
            gat[h, j * 256 : (j + 1) * 256, :] = live.astype(BF)
        loads = srcf[:, es] - dot(cip[...], gat[h])
        loads = jnp.where(inner_live[:, es], loads, 0.0)
        lo_all[h, f, 0:176] = jnp.concatenate([loads, zero8], axis=0).astype(BF)
        for dev in field_peers:
            ex2[h].append(send(lo_all.at[h, f, pl.ds(0, 176)], lo_all.at[h, f, pl.ds(0, 176)], dev))
    for c in dz:
        c.wait_recv()
    for c in range(2):
        r2[y, c] = r1[:, c, :]
    dy = []
    for i in range(1, 8):
        dy.append(send(r2.at[y], r2.at[y], y_peers[i - 1]))

    colw = iota((672, PADK), 1)
    slab = (colw >= 192).astype(I32) + (colw >= 384).astype(I32) + (colw >= 576).astype(I32)
    inn = colw - slab * 192
    perms = one_hot(iota((672, PADK), 0) == jnp.where(inn < 168, slab * 168 + inn, -1))
    fetch[7].wait()
    lip[...] = dot(liv[...], perms).astype(BF)
    fetch[8].wait()
    cop[...] = dot(dot(permr, cov[...]).astype(BF), perms).astype(BF)
    for h in range(2):
        tbg[h] = dot(tbp[...], gat[h])

    ex3 = [[], []]
    for h in range(2):
        es = slice(h * HE, h * HE + HE)
        for c in ex2[h]:
            c.wait_recv()
        inter = dot(lip[...], lo_all[h].reshape(PADK, HE))
        inter = jnp.where(inner_live[:, es], inter, 0.0)
        in_all[h, f, 0:176] = jnp.concatenate([inter, zero8], axis=0).astype(BF)
        for dev in field_peers:
            ex3[h].append(send(in_all.at[h, f, pl.ds(0, 176)], in_all.at[h, f, pl.ds(0, 176)], dev))
    for c in dy:
        c.wait_recv()
    dk = send(r2, r3.at[k], core_peer)
    r3[k] = r2[...]

    fetch[9].wait()
    slots = slot_ref[...]
    parts = jnp.concatenate([(slots >> 4).astype(F32), (slots & 15).astype(F32)] + [jnp.zeros((6, FACES), F32)], axis=0)
    cs = iota((FACES, FACES), 1)
    spread = one_hot(iota((FACES, FACES), 0) == (cs & 127) * 4 + (cs >> 7))
    moved = dot(parts.astype(BF), spread).astype(I32)
    slot_qt = moved[0:1] * 16 + moved[1:2]
    pm[...] = one_hot(iota((FACES, FACES), 0) == slot_qt)

    fetch[10].wait()
    fetch[11].wait()
    acc = jnp.zeros((2 * CK, EXT), F32)
    for h in range(2):
        es = slice(h * HE, h * HE + HE)
        for c in ex3[h]:
            c.wait_recv()
        blocks = tbg[h] + dot(cop[...], in_all[h].reshape(PADK, HE))
        blocks = jnp.where(face_live[:, es], blocks, 0.0) * scl_ref[:, es]
        wide = jnp.concatenate([blocks[j * CK : (j + 1) * CK] for j in range(4)], axis=1)
        acc = acc + dot_nt(hi_lo(wide), oh[:, h * 512 : h * 512 + 512])
    res = acc[0:CK] + acc[CK : 2 * CK]
    ownres[...] = res[:, 0:FACES]
    rim4[0] = packed_rim(res[:, FACES:EXT], 0).astype(BF)
    rim4[1] = packed_rim(res[:, FACES:EXT], RIM).astype(BF)
    ra[f] = res[:, 0:FACES].astype(BF)

    ex4 = []
    for dev in prev_all:
        ex4.append(send(rim4.at[0], xr4.at[0, f], dev))
    for dev in next_all:
        ex4.append(send(rim4.at[1], xr4.at[1, f], dev))
    for dev in field_peers:
        ex4.append(send(ra.at[f], ra.at[f], dev))

    dk.wait_recv()
    r_i = iota((128, 128), 0)
    t_of = (r_i & 7) * 16 + ((r_i >> 3) & 7) * 2 + (r_i >> 6)
    to_t = one_hot(iota((128, 128), 1) == t_of)
    for c in range(2):
        dt[c] = r3[:, :, c].reshape(128, 128).T
    start = 3 + 4 * (d % 16)
    lane = iota((1, 128), 1)
    for c in range(2):
        win = dt[c, pl.ds(start, 16), :]
        w0 = win.astype(BF)
        rest = win - w0.astype(F32)
        w1 = rest.astype(BF)
        w2 = (rest - w1.astype(F32)).astype(BF)
        got = dot(jnp.concatenate([w0, w1, w2], axis=0), to_t)
        dwin[c] = 1.0 / (got[0:16] + got[16:32] + got[32:48])

    def shifted(v, wrap, step):
        edge = 0 if step == 1 else 127
        rolled = jnp.where(lane == edge, 0.0, pltpu.roll(v, step % 128, 1))
        return jnp.where(wrap, rolled, v)

    wraps = [d <= 1] + [d == 0] * 4 + [None] * 4 + [d == ND - 1] * 4 + [d >= ND - 2]

    def placed(v, i):
        if i < 5:
            return shifted(v, wraps[i], 1)
        if i > 8:
            return shifted(v, wraps[i], -1)
        return v

    inv = []
    for c in range(2):
        inv.append([placed(jnp.broadcast_to(dwin[c, i : i + 1, :], (8, 128)), i) for i in range(14)])

    for c in ex4:
        c.wait_recv()

    mine = ownres[...]
    mixed = [None, None]
    for g in range(NF):
        whole = jnp.where(f == g, mine, ra[g].astype(F32))
        whole = jnp.concatenate(
            [
                whole[:, 0:128] + unpacked_rim(xr4[1, g].astype(F32), 0),
                whole[:, 128:384],
                whole[:, 384:512] + unpacked_rim(xr4[0, g].astype(F32), 96),
            ],
            axis=1,
        )
        for cc in range(2):
            part = whole[cc * 32 : cc * 32 + 32]
            for c in range(2):
                coef = mix_ref[c : c + 1, 2 * g + cc : 2 * g + cc + 1]
                coef = coef + jnp.where((f == g) & (c == cc), 1.0, 0.0)
                term = coef * part
                mixed[c] = term if mixed[c] is None else mixed[c] + term
    both = jnp.concatenate(mixed, axis=0)
    moved_rhs = dot(hi_lo(both), pm[...])
    rhs = moved_rhs[0:CK] + moved_rhs[CK : 2 * CK]
    vb[...] = rhs.astype(BF)

    ex5 = [
        send(vb, ln, (dom_at(1), f)),
        send(vb, rn, (dom_at(-1), f)),
        send(vb.at[:, pl.ds(384, 128)], ll, far[0]),
        send(vb.at[:, pl.ds(0, 128)], rr, far[1]),
    ]
    for c in range(2):
        mixed_ref[c] = mixed[c][0:NFD]
    for c in ex5:
        c.wait_recv()

    corr = []
    for b in range(8):
        rows = slice(b * 8, b * 8 + 8)
        iv = inv[b // 4]
        pair = slice((b // 2) * 16, (b // 2) * 16 + 16)
        half = slice((b % 2) * 8, (b % 2) * 8 + 8)

        def get(ref, q):
            return ref[pair, q * 128 : (q + 1) * 128].astype(F32)[half]

        r = [get(ll, 0)] + [get(ln, q) for q in range(4)] + [rhs[rows, q * 128 : (q + 1) * 128] for q in range(4)]
        r = r + [get(rn, q) for q in range(4)] + [get(rr, 0)]
        yv = {i: iv[i] * placed(r[i], i) for i in range(14)}

        def residual(yy, zz, lo, hi):
            return {i: yy[i] + iv[i] * (zz[i - 1] + zz[i + 1]) - zz[i] for i in range(lo, hi)}

        def sweep(yy, lo, hi):
            step = dict(yy)
            total = dict(yy)
            rho = RHO0
            for _ in range(2):
                lo, hi = lo + 1, hi - 1
                rho_next = 1.0 / (2.0 * RATIO - rho)
                u = residual(yy, total, lo, hi)
                step = {i: (rho_next * rho) * step[i] + (2.0 * rho_next / HALF) * u[i] for i in range(lo, hi)}
                total = {i: total[i] + step[i] for i in range(lo, hi)}
                rho = rho_next
            return total, lo, hi

        first, lo, hi = sweep(yv, 0, 14)
        y2 = residual(yv, first, lo + 1, hi - 1)
        second, lo, hi = sweep(y2, lo + 1, hi - 1)
        corr.append(jnp.concatenate([first[i] + second[i] for i in range(5, 9)], axis=1))
    corr = jnp.concatenate(corr, axis=0)
    back = dot_nt(hi_lo(corr), pm[...])
    new = own32[...] - (back[0:CK] + back[CK : 2 * CK])
    for c in range(2):
        new_ref[c] = new[c * 32 : c * 32 + NFD]
    for c in sent:
        c.wait_send()


def shards(
    traces,
    interior_source,
    orders,
    element_scale,
    element_faces,
    solver_slots,
    line_diagonal,
    species_mix,
    couple_in,
    local_inverse,
    trace_block,
    couple_out,
):
    vmem = pl.BlockSpec(memory_space=pltpu.VMEM)
    hbm = pl.BlockSpec(memory_space=pltpu.HBM)
    n_copies = 64
    scratch = [
        pltpu.VMEM((NF, CK, EXT), BF),
        pltpu.VMEM((EXT, 1024), BF),
        pltpu.VMEM((2, 1024, HE), BF),
        pltpu.VMEM((168, 896), BF),
        pltpu.VMEM((168, 672), BF),
        pltpu.VMEM((224, 896), BF),
        pltpu.VMEM((224, 672), BF),
        pltpu.VMEM((168, 1024), BF),
        pltpu.VMEM((168, PADK), BF),
        pltpu.VMEM((256, 1024), BF),
        pltpu.VMEM((256, PADK), BF),
        pltpu.VMEM((168, ELEMS), F32),
        pltpu.VMEM((2, NF, 192, HE), BF),
        pltpu.VMEM((2, NF, 192, HE), BF),
        pltpu.VMEM((NF, CK, FACES), BF),
        pltpu.VMEM((2, 16, 128), BF),
        pltpu.VMEM((2, NF, 16, 128), BF),
        pltpu.VMEM((2, 16, 128), BF),
        pltpu.VMEM((2, NF, 16, 128), BF),
        pltpu.VMEM((CK, FACES), BF),
        pltpu.VMEM((CK, FACES), BF),
        pltpu.VMEM((CK, FACES), BF),
        pltpu.VMEM((CK, 128), BF),
        pltpu.VMEM((CK, 128), BF),
        pltpu.VMEM((8, 2, 128), F32),
        pltpu.VMEM((8, 2, 128), F32),
        pltpu.VMEM((8, 2, 8, 128), F32),
        pltpu.VMEM((2, 8, 2, 8, 128), F32),
        pltpu.VMEM((2, 128, 128), F32),
        pltpu.VMEM((2, 16, 128), F32),
        pltpu.VMEM((FACES, FACES), BF),
        pltpu.VMEM((CK, FACES), F32),
        pltpu.VMEM((2, 256, HE), F32),
        pltpu.VMEM((CK, FACES), F32),
        pltpu.VMEM((2, FACES), F32),
        pltpu.VMEM((NFD, 2, FACES), F32),
        pltpu.VMEM((4, ELEMS), I32),
        pltpu.VMEM((1, ELEMS), I32),
        pltpu.VMEM((NID, 2, ELEMS), BF),
        pltpu.VMEM((1, FACES), I32),
        pltpu.VMEM((1, ELEMS), F32),
        pltpu.VMEM((2, 8), F32),
        pltpu.SemaphoreType.DMA((12,)),
        pltpu.SemaphoreType.DMA((n_copies,)),
        pltpu.SemaphoreType.DMA((n_copies,)),
    ]
    shape = jax.ShapeDtypeStruct((2, NFD, FACES), F32)
    new, mixed = pl.pallas_call(
        kernel,
        out_shape=(shape, shape),
        in_specs=[hbm] * 12,
        out_specs=(vmem, vmem),
        scratch_shapes=scratch,
        compiler_params=pltpu.CompilerParams(
            collective_id=0, has_side_effects=True, vmem_limit_bytes=48 * 1024 * 1024
        ),
    )(
        pltpu.with_memory_space_constraint(line_diagonal, pltpu.HBM),
        pltpu.with_memory_space_constraint(jnp.transpose(traces, (1, 0, 2)), pltpu.HBM),
        pltpu.with_memory_space_constraint(element_faces, pltpu.HBM),
        pltpu.with_memory_space_constraint(orders.reshape(1, ELEMS), pltpu.HBM),
        pltpu.with_memory_space_constraint(jnp.transpose(interior_source, (1, 0, 2)), pltpu.HBM),
        pltpu.with_memory_space_constraint(couple_in, pltpu.HBM),
        pltpu.with_memory_space_constraint(trace_block, pltpu.HBM),
        pltpu.with_memory_space_constraint(local_inverse, pltpu.HBM),
        pltpu.with_memory_space_constraint(couple_out, pltpu.HBM),
        pltpu.with_memory_space_constraint(solver_slots.reshape(1, FACES), pltpu.HBM),
        pltpu.with_memory_space_constraint(element_scale.reshape(1, ELEMS), pltpu.HBM),
        pltpu.with_memory_space_constraint(species_mix, pltpu.HBM),
    )
    return new, mixed


def solution(mesh):
    in_specs = (
        P("field", None, "dom"),
        P("field", None, "dom"),
        P("dom"),
        P("dom"),
        P(None, "dom"),
        P("dom"),
        P("field", "dom"),
        P("field", None),
        P("field", None),
        P("field", None),
        P("field", None),
        P("field", None),
    )
    out_specs = (P("field", None, "dom"), P("field", None, "dom"))
    return jax.shard_map(shards, mesh=mesh, in_specs=in_specs, out_specs=out_specs, check_vma=False)
```

```python
import functools

import jax
import jax.numpy as jnp
from jax import lax
from jax.experimental import pallas as pl
from jax.experimental.pallas import tpu as pltpu
from jax.sharding import PartitionSpec as P

F32 = jnp.float32
BF = jnp.bfloat16
I32 = jnp.int32
MESH = pl.DeviceIdType.MESH

NFD = 28
NID = 84
ND = 128
NF = 4
FACES = 512
ELEMS = 256
CK = 64
EXT = 640
PADK = 768
HE = 128
RIM = 32
RHO0 = 0.8
HALF = 0.8
RATIO = 1.25


def dot(a, b):
    return jnp.dot(a, b, preferred_element_type=F32)


def dot_nt(a, b):
    return lax.dot_general(a, b, (((1,), (1,)), ((), ())), preferred_element_type=F32)


def iota(shape, dim):
    return lax.broadcasted_iota(I32, shape, dim)


def one_hot(cond):
    return jnp.where(cond, 1.0, 0.0).astype(BF)


def hi_lo(x):
    hi = x.astype(BF)
    lo = (x - hi.astype(F32)).astype(BF)
    return jnp.concatenate([hi, lo], axis=0)


def packed_rim(x, lane0):
    lane = iota((16, 128), 1)
    out = jnp.zeros((16, 128), F32)
    for i in range(4):
        part = pltpu.roll(x[16 * i : 16 * i + 16], (RIM * i - lane0) % 128, 1)
        out = jnp.where((lane >= RIM * i) & (lane < RIM * i + RIM), part, out)
    return out


def unpacked_rim(x, lane0):
    lane = iota((16, 128), 1)
    keep = (lane >= lane0) & (lane < lane0 + RIM)
    parts = [jnp.where(keep, pltpu.roll(x, (lane0 - RIM * i) % 128, 1), 0.0) for i in range(4)]
    return jnp.concatenate(parts, axis=0)


def kernel(
    dia_hbm, tr_hbm, fac_hbm, ord_hbm, src_hbm, ci_hbm, tb_hbm, li_hbm, co_hbm, slot_hbm, scl_hbm, mix_hbm,
    new_ref, mixed_ref,
    ta, oh, gat, civ, liv, tbv, cov, cip, lip, tbp, cop, cocol, srcf,
    lo_all, mp, sb, rb, rim1, xr1, rim4, xr4, vb, ln, rn, ll, rr,
    s1, r1, r2, r3, dt, dwin, pm, own32, tbg,
    dia_ref, tr_ref, fac_ref, ord_ref, src_ref, slot_ref, scl_ref, mix_ref,
    wsem, ssem, rsem,
):
    d = lax.axis_index("dom")
    f = lax.axis_index("field")
    z = d // 16
    y = (d % 16) // 2
    k = d % 2

    def dom_at(step):
        return (d + step + ND) % ND

    def field_at(step):
        return (f + step) % NF

    pairs = (
        (tr_hbm, tr_ref), (dia_hbm, dia_ref), (fac_hbm, fac_ref), (ord_hbm, ord_ref), (src_hbm, src_ref),
        (ci_hbm, civ), (tb_hbm, tbv), (li_hbm, liv), (co_hbm, cov),
        (slot_hbm, slot_ref), (scl_hbm, scl_ref), (mix_hbm, mix_ref.at[f]),
    )
    fetch = [pltpu.make_async_copy(src, dst, wsem.at[i]) for i, (src, dst) in enumerate(pairs)]
    for c in fetch:
        c.start()

    field_peers = [(d, field_at(i)) for i in range(1, NF)]
    next_all = [(dom_at(1), field_at(i)) for i in range(NF)]
    prev_all = [(dom_at(-1), field_at(i)) for i in range(NF)]
    far = [(dom_at(2), f), (dom_at(-2), f)]
    z_peers = [(((z + i) % 8) * 16 + d % 16, f) for i in range(1, 8)]
    y_peers = [(z * 16 + ((y + i) % 8) * 2 + k, f) for i in range(1, 8)]
    core_peer = (d + 1 - 2 * k, f)
    greet = field_peers + next_all + prev_all + far + z_peers + y_peers
    barrier = pltpu.get_barrier_semaphore()
    for dev in greet:
        pl.semaphore_signal(barrier, inc=1, device_id=dev, device_id_type=MESH)

    count = [0]
    sent = []

    def send(src, dst, dev):
        n = count[0]
        count[0] += 1
        c = pltpu.make_async_remote_copy(
            src_ref=src, dst_ref=dst, send_sem=ssem.at[n], recv_sem=rsem.at[n],
            device_id=dev, device_id_type=MESH,
        )
        c.start()
        sent.append(c)
        return c

    pad16 = jnp.zeros((16, HE), BF)
    for g in range(NF):
        for h in range(2):
            lo_all[h, g, 176:192, :] = pad16

    own32[...] = jnp.zeros((CK, FACES), F32)
    fetch[0].wait()
    for c in range(2):
        own32[c * 32 : c * 32 + NFD, :] = tr_ref[:, c, :]
    ta[f, :, 0:FACES] = own32[...].astype(BF)
    rim1[0] = packed_rim(own32[:, 0:128], 0).astype(BF)
    rim1[1] = packed_rim(own32[:, 384:512], 96).astype(BF)
    pl.semaphore_wait(barrier, len(greet))

    ex1 = []
    for dev in next_all:
        ex1.append(send(rim1.at[1], xr1.at[0, f], dev))
    for dev in prev_all:
        ex1.append(send(rim1.at[0], xr1.at[1, f], dev))
    for dev in field_peers:
        ex1.append(send(ta.at[f, :, pl.ds(0, FACES)], ta.at[f, :, pl.ds(0, FACES)], dev))
    fetch[11].wait()
    exm = [send(mix_ref.at[f], mix_ref.at[f], dev) for dev in field_peers]
    fetch[1].wait()
    dia = jnp.concatenate([dia_ref[...]] * 4, axis=0)
    for zz in range(8):
        s1[zz] = pltpu.roll(dia, (8 - 64 * zz) % FACES, 1)[0:2, 0:128]
    dz = []
    for i in range(1, 8):
        dz.append(send(s1.at[(z + i) % 8], r1.at[z], z_peers[i - 1]))
    r1[z] = s1[z]

    rown = iota((256, 224), 0)
    rk = rown & 31
    want_r = jnp.where(rk < NFD, ((rown >> 5) & 1) * 112 + (rown >> 6) * NFD + rk, -1)
    permr = one_hot(iota((256, 224), 1) == want_r)
    colw = iota((672, 1024), 1)
    inn = colw & 255
    permw = one_hot(iota((672, 1024), 0) == jnp.where(inn < 168, (colw >> 8) * 168 + inn, -1))
    fetch[8].wait()
    wide = dot(dot(permr, cov[...]).astype(BF), permw).astype(BF)
    for g in range(NF):
        cop[g] = wide[:, g * 256 : (g + 1) * 256]
    half_rows = pl.ds(pl.multiple_of(k * 128, 128), 128)
    exw = []
    for i in range(1, NF):
        exw.append(send(cop.at[field_at(i), half_rows], cocol.at[f, half_rows], field_peers[i - 1]))
    cocol[f] = cop[f]

    fetch[2].wait()
    rel = (fac_ref[...] - d * FACES) & (ND * FACES - 1)
    lid = jnp.where(
        rel < FACES, rel, jnp.where(rel >= ND * FACES - RIM, rel - (ND * FACES - RIM) + FACES, rel + RIM)
    )
    for h in range(2):
        for j in range(4):
            c0 = h * 512 + j * HE
            oh[:, c0 : c0 + HE] = one_hot(iota((EXT, HE), 0) == lid[j : j + 1, h * HE : h * HE + HE])
    fetch[3].wait()
    order = ord_ref[...]
    face_n = (order + 1) * (order + 2)
    inner_n = face_n * (order + 3)
    face_live = 2 * (iota((256, ELEMS), 0) & 31) < face_n
    row = iota((2 * NID, ELEMS), 0)
    inner_live = 6 * jnp.where(row >= NID, row - NID, row) < inner_n
    fetch[4].wait()
    for c in range(2):
        srcf[c * NID : (c + 1) * NID, :] = src_ref[:, c, :].astype(F32)
    zero8 = jnp.zeros((8, HE), F32)

    col = iota((896, 1024), 1)
    kk = col & 31
    want = jnp.where(kk < NFD, ((col >> 5) & 7) * 112 + (col >> 8) * NFD + kk, -1)
    permk = one_hot(iota((896, 1024), 0) == want)
    fetch[5].wait()
    cip[...] = dot(civ[...], permk).astype(BF)
    fetch[6].wait()
    tbp[...] = dot(dot(permr, tbv[...]).astype(BF), permk).astype(BF)

    for c in ex1:
        c.wait_recv()
    for g in range(NF):
        ta[g, :, FACES:EXT] = (
            unpacked_rim(xr1[0, g].astype(F32), 0) + unpacked_rim(xr1[1, g].astype(F32), RIM)
        ).astype(BF)
    tall = ta[...].reshape(256, EXT)
    ex2 = [[], []]
    for h in range(2):
        es = slice(h * HE, h * HE + HE)
        picked = dot(tall, oh[:, h * 512 : h * 512 + 512])
        for j in range(4):
            live = jnp.where(face_live[:, es], picked[:, j * HE : (j + 1) * HE], 0.0)
            gat[h, j * 256 : (j + 1) * 256, :] = live.astype(BF)
        loads = srcf[:, es] - dot(cip[...], gat[h])
        loads = jnp.where(inner_live[:, es], loads, 0.0)
        lo_all[h, f, 0:176] = jnp.concatenate([loads, zero8], axis=0).astype(BF)
        for dev in field_peers:
            ex2[h].append(send(lo_all.at[h, f, pl.ds(0, 176)], lo_all.at[h, f, pl.ds(0, 176)], dev))
    for c in exw:
        c.wait_recv()
    exf = []
    for i in range(1, NF):
        part = cocol.at[field_at(i), half_rows]
        exf.append(send(part, part, core_peer))
    for c in dz:
        c.wait_recv()
    for c in range(2):
        r2[y, c] = r1[:, c, :]
    dy = []
    for i in range(1, 8):
        dy.append(send(r2.at[y], r2.at[y], y_peers[i - 1]))

    colw = iota((672, PADK), 1)
    slab = (colw >= 192).astype(I32) + (colw >= 384).astype(I32) + (colw >= 576).astype(I32)
    inn = colw - slab * 192
    perms = one_hot(iota((672, PADK), 0) == jnp.where(inn < 168, slab * 168 + inn, -1))
    fetch[7].wait()
    lip[...] = dot(liv[...], perms).astype(BF)
    for h in range(2):
        tbg[h] = dot(tbp[...], gat[h])

    for c in exf:
        c.wait_recv()
    fetch[10].wait()
    zero88 = jnp.zeros((88, HE), F32)
    acc = None
    for h in range(2):
        es = slice(h * HE, h * HE + HE)
        for c in ex2[h]:
            c.wait_recv()
        inter = dot(lip[...], lo_all[h].reshape(PADK, HE))
        inter = jnp.where(inner_live[:, es], inter, 0.0)
        inter = jnp.concatenate([inter, zero88], axis=0).astype(BF)
        his, los = [], []
        for g in range(NF):
            blocks = dot(cocol[g], inter) + jnp.where(f == g, tbg[h], 0.0)
            blocks = jnp.where(face_live[:, es], blocks, 0.0) * scl_ref[:, es]
            flat = jnp.concatenate([blocks[j * CK : (j + 1) * CK] for j in range(4)], axis=1)
            hi = flat.astype(BF)
            his.append(hi)
            los.append((flat - hi.astype(F32)).astype(BF))
        part = dot_nt(jnp.concatenate(his + los, axis=0), oh[:, h * 512 : h * 512 + 512])
        acc = part if acc is None else acc + part
    res = acc[0:256] + acc[256:512]

    for c in exm:
        c.wait_recv()
    for c in range(8):
        share = res[c * 32 : c * 32 + 32]
        for c2 in range(8):
            share = share + mix_ref[c // 2, c % 2 : c % 2 + 1, c2 : c2 + 1] * res[c2 * 32 : c2 * 32 + 32]
        mp[c // 2, (c % 2) * 32 : (c % 2) * 32 + 32, :] = share
    for g in range(NF):
        sb[g] = mp[g, :, 0:FACES].astype(BF)
        rim = mp[g, :, FACES:EXT]
        rim4[g, 0] = packed_rim(rim, 0).astype(BF)
        rim4[g, 1] = packed_rim(rim, RIM).astype(BF)

    ex4 = []
    for i in range(NF):
        ex4.append(send(rim4.at[field_at(i), 0], xr4.at[0, f], prev_all[i]))
        ex4.append(send(rim4.at[field_at(i), 1], xr4.at[1, f], next_all[i]))
    for i in range(1, NF):
        ex4.append(send(sb.at[field_at(i)], rb.at[f], field_peers[i - 1]))

    for c in dy:
        c.wait_recv()
    dk = send(r2, r3.at[k], core_peer)
    r3[k] = r2[...]

    fetch[9].wait()
    slots = slot_ref[...]
    parts = jnp.concatenate([(slots >> 4).astype(F32), (slots & 15).astype(F32)] + [jnp.zeros((6, FACES), F32)], axis=0)
    cs = iota((FACES, FACES), 1)
    spread = one_hot(iota((FACES, FACES), 0) == (cs & 127) * 4 + (cs >> 7))
    moved = dot(parts.astype(BF), spread).astype(I32)
    slot_qt = moved[0:1] * 16 + moved[1:2]
    pm[...] = one_hot(iota((FACES, FACES), 0) == slot_qt)

    dk.wait_recv()
    r_i = iota((128, 128), 0)
    t_of = (r_i & 7) * 16 + ((r_i >> 3) & 7) * 2 + (r_i >> 6)
    to_t = one_hot(iota((128, 128), 1) == t_of)
    for c in range(2):
        dt[c] = r3[:, :, c].reshape(128, 128).T
    start = 3 + 4 * (d % 16)
    lane = iota((1, 128), 1)
    for c in range(2):
        win = dt[c, pl.ds(start, 16), :]
        w0 = win.astype(BF)
        rest = win - w0.astype(F32)
        w1 = rest.astype(BF)
        w2 = (rest - w1.astype(F32)).astype(BF)
        got = dot(jnp.concatenate([w0, w1, w2], axis=0), to_t)
        dwin[c] = 1.0 / (got[0:16] + got[16:32] + got[32:48])

    def shifted(v, wrap, step):
        edge = 0 if step == 1 else 127
        rolled = jnp.where(lane == edge, 0.0, pltpu.roll(v, step % 128, 1))
        return jnp.where(wrap, rolled, v)

    wraps = [d <= 1] + [d == 0] * 4 + [None] * 4 + [d == ND - 1] * 4 + [d >= ND - 2]

    def placed(v, i):
        if i < 5:
            return shifted(v, wraps[i], 1)
        if i > 8:
            return shifted(v, wraps[i], -1)
        return v

    inv = []
    for c in range(2):
        inv.append([placed(jnp.broadcast_to(dwin[c, i : i + 1, :], (8, 128)), i) for i in range(14)])

    for c in ex4:
        c.wait_recv()

    both = mp[f, :, 0:FACES]
    for i in range(1, NF):
        both = both + rb[field_at(i)].astype(F32)
    to_last = sum(xr4[0, g].astype(F32) for g in range(NF))
    to_first = sum(xr4[1, g].astype(F32) for g in range(NF))
    both = jnp.concatenate(
        [
            both[:, 0:128] + unpacked_rim(to_first, 0),
            both[:, 128:384],
            both[:, 384:512] + unpacked_rim(to_last, 96),
        ],
        axis=1,
    )
    moved_rhs = dot(hi_lo(both), pm[...])
    rhs = moved_rhs[0:CK] + moved_rhs[CK : 2 * CK]
    vb[...] = rhs.astype(BF)

    ex5 = [
        send(vb, ln, (dom_at(1), f)),
        send(vb, rn, (dom_at(-1), f)),
        send(vb.at[:, pl.ds(384, 128)], ll, far[0]),
        send(vb.at[:, pl.ds(0, 128)], rr, far[1]),
    ]
    for c in range(2):
        mixed_ref[c] = both[c * 32 : c * 32 + NFD]
    for c in ex5:
        c.wait_recv()

    corr = []
    for b in range(8):
        rows = slice(b * 8, b * 8 + 8)
        iv = inv[b // 4]
        pair = slice((b // 2) * 16, (b // 2) * 16 + 16)
        half = slice((b % 2) * 8, (b % 2) * 8 + 8)

        def get(ref, q):
            return ref[pair, q * 128 : (q + 1) * 128].astype(F32)[half]

        r = [get(ll, 0)] + [get(ln, q) for q in range(4)] + [rhs[rows, q * 128 : (q + 1) * 128] for q in range(4)]
        r = r + [get(rn, q) for q in range(4)] + [get(rr, 0)]
        yv = {i: iv[i] * placed(r[i], i) for i in range(14)}

        def residual(yy, zz, lo, hi):
            return {i: yy[i] + iv[i] * (zz[i - 1] + zz[i + 1]) - zz[i] for i in range(lo, hi)}

        def sweep(yy, lo, hi):
            step = dict(yy)
            total = dict(yy)
            rho = RHO0
            for _ in range(2):
                lo, hi = lo + 1, hi - 1
                rho_next = 1.0 / (2.0 * RATIO - rho)
                u = residual(yy, total, lo, hi)
                step = {i: (rho_next * rho) * step[i] + (2.0 * rho_next / HALF) * u[i] for i in range(lo, hi)}
                total = {i: total[i] + step[i] for i in range(lo, hi)}
                rho = rho_next
            return total, lo, hi

        first, lo, hi = sweep(yv, 0, 14)
        y2 = residual(yv, first, lo + 1, hi - 1)
        second, lo, hi = sweep(y2, lo + 1, hi - 1)
        corr.append(jnp.concatenate([first[i] + second[i] for i in range(5, 9)], axis=1))
    corr = jnp.concatenate(corr, axis=0)
    back = dot_nt(hi_lo(corr), pm[...])
    new = own32[...] - (back[0:CK] + back[CK : 2 * CK])
    for c in range(2):
        new_ref[c] = new[c * 32 : c * 32 + NFD]
    for c in sent:
        c.wait_send()


def shards(
    traces,
    interior_source,
    orders,
    element_scale,
    element_faces,
    solver_slots,
    line_diagonal,
    species_mix,
    couple_in,
    local_inverse,
    trace_block,
    couple_out,
):
    vmem = pl.BlockSpec(memory_space=pltpu.VMEM)
    hbm = pl.BlockSpec(memory_space=pltpu.HBM)
    n_copies = 64
    scratch = [
        pltpu.VMEM((NF, CK, EXT), BF),
        pltpu.VMEM((EXT, 1024), BF),
        pltpu.VMEM((2, 1024, HE), BF),
        pltpu.VMEM((168, 896), BF),
        pltpu.VMEM((168, 672), BF),
        pltpu.VMEM((224, 896), BF),
        pltpu.VMEM((224, 672), BF),
        pltpu.VMEM((168, 1024), BF),
        pltpu.VMEM((168, PADK), BF),
        pltpu.VMEM((256, 1024), BF),
        pltpu.VMEM((NF, 256, 256), BF),
        pltpu.VMEM((NF, 256, 256), BF),
        pltpu.VMEM((168, ELEMS), F32),
        pltpu.VMEM((2, NF, 192, HE), BF),
        pltpu.VMEM((NF, CK, EXT), F32),
        pltpu.VMEM((NF, CK, FACES), BF),
        pltpu.VMEM((NF, CK, FACES), BF),
        pltpu.VMEM((2, 16, 128), BF),
        pltpu.VMEM((2, NF, 16, 128), BF),
        pltpu.VMEM((NF, 2, 16, 128), BF),
        pltpu.VMEM((2, NF, 16, 128), BF),
        pltpu.VMEM((CK, FACES), BF),
        pltpu.VMEM((CK, FACES), BF),
        pltpu.VMEM((CK, FACES), BF),
        pltpu.VMEM((CK, 128), BF),
        pltpu.VMEM((CK, 128), BF),
        pltpu.VMEM((8, 2, 128), F32),
        pltpu.VMEM((8, 2, 128), F32),
        pltpu.VMEM((8, 2, 8, 128), F32),
        pltpu.VMEM((2, 8, 2, 8, 128), F32),
        pltpu.VMEM((2, 128, 128), F32),
        pltpu.VMEM((2, 16, 128), F32),
        pltpu.VMEM((FACES, FACES), BF),
        pltpu.VMEM((CK, FACES), F32),
        pltpu.VMEM((2, 256, HE), F32),
        pltpu.VMEM((2, FACES), F32),
        pltpu.VMEM((NFD, 2, FACES), F32),
        pltpu.VMEM((4, ELEMS), I32),
        pltpu.VMEM((1, ELEMS), I32),
        pltpu.VMEM((NID, 2, ELEMS), BF),
        pltpu.VMEM((1, FACES), I32),
        pltpu.VMEM((1, ELEMS), F32),
        pltpu.VMEM((NF, 2, 8), F32),
        pltpu.SemaphoreType.DMA((12,)),
        pltpu.SemaphoreType.DMA((n_copies,)),
        pltpu.SemaphoreType.DMA((n_copies,)),
    ]
    shape = jax.ShapeDtypeStruct((2, NFD, FACES), F32)
    new, mixed = pl.pallas_call(
        kernel,
        out_shape=(shape, shape),
        in_specs=[hbm] * 12,
        out_specs=(vmem, vmem),
        scratch_shapes=scratch,
        compiler_params=pltpu.CompilerParams(
            collective_id=0, has_side_effects=True, vmem_limit_bytes=48 * 1024 * 1024
        ),
    )(
        pltpu.with_memory_space_constraint(line_diagonal, pltpu.HBM),
        pltpu.with_memory_space_constraint(jnp.transpose(traces, (1, 0, 2)), pltpu.HBM),
        pltpu.with_memory_space_constraint(element_faces, pltpu.HBM),
        pltpu.with_memory_space_constraint(orders.reshape(1, ELEMS), pltpu.HBM),
        pltpu.with_memory_space_constraint(jnp.transpose(interior_source, (1, 0, 2)), pltpu.HBM),
        pltpu.with_memory_space_constraint(couple_in, pltpu.HBM),
        pltpu.with_memory_space_constraint(trace_block, pltpu.HBM),
        pltpu.with_memory_space_constraint(local_inverse, pltpu.HBM),
        pltpu.with_memory_space_constraint(couple_out, pltpu.HBM),
        pltpu.with_memory_space_constraint(solver_slots.reshape(1, FACES), pltpu.HBM),
        pltpu.with_memory_space_constraint(element_scale.reshape(1, ELEMS), pltpu.HBM),
        pltpu.with_memory_space_constraint(species_mix, pltpu.HBM),
    )
    return new, mixed


def solution(mesh):
    in_specs = (
        P("field", None, "dom"),
        P("field", None, "dom"),
        P("dom"),
        P("dom"),
        P(None, "dom"),
        P("dom"),
        P("field", "dom"),
        P("field", None),
        P("field", None),
        P("field", None),
        P("field", None),
        P("field", None),
    )
    out_specs = (P("field", None, "dom"), P("field", None, "dom"))
    return jax.shard_map(shards, mesh=mesh, in_specs=in_specs, out_specs=out_specs, check_vma=False)
```

```python
import functools

import jax
import jax.numpy as jnp
from jax import lax
from jax.experimental import pallas as pl
from jax.experimental.pallas import tpu as pltpu
from jax.sharding import PartitionSpec as P

F32 = jnp.float32
BF = jnp.bfloat16
I32 = jnp.int32
MESH = pl.DeviceIdType.MESH

NFD = 28
NID = 84
ND = 128
NF = 4
FACES = 512
ELEMS = 256
CK = 64
EXT = 640
PADK = 768
HE = 128
RIM = 32
RHO0 = 0.8
HALF = 0.8
RATIO = 1.25


def dot(a, b):
    return jnp.dot(a, b, preferred_element_type=F32)


def dot_nt(a, b):
    return lax.dot_general(a, b, (((1,), (1,)), ((), ())), preferred_element_type=F32)


def iota(shape, dim):
    return lax.broadcasted_iota(I32, shape, dim)


def one_hot(cond):
    return jnp.where(cond, 1.0, 0.0).astype(BF)


def hi_lo(x):
    hi = x.astype(BF)
    lo = (x - hi.astype(F32)).astype(BF)
    return jnp.concatenate([hi, lo], axis=0)


def packed_rim(x, lane0):
    lane = iota((16, 128), 1)
    out = jnp.zeros((16, 128), F32)
    for i in range(4):
        part = pltpu.roll(x[16 * i : 16 * i + 16], (RIM * i - lane0) % 128, 1)
        out = jnp.where((lane >= RIM * i) & (lane < RIM * i + RIM), part, out)
    return out


def unpacked_rim(x, lane0):
    lane = iota((16, 128), 1)
    keep = (lane >= lane0) & (lane < lane0 + RIM)
    parts = [jnp.where(keep, pltpu.roll(x, (lane0 - RIM * i) % 128, 1), 0.0) for i in range(4)]
    return jnp.concatenate(parts, axis=0)


def kernel(
    dia_hbm, tr_hbm, fac_hbm, ord_hbm, src_hbm, ci_hbm, tb_hbm, li_hbm, co_hbm, slot_hbm, scl_hbm, mix_hbm,
    new_ref, mixed_ref,
    ta, oh, gat, civ, liv, tbv, cov, cip, lip, tbp, cop, cocol, srcf,
    lo_all, mp, sb, rb, rim1, xr1, rim4, xr4, vb, ln, rn, ll, rr,
    s1, r1, r2, r3, dt, dwin, pm, own32, tbg, cf,
    dia_ref, tr_ref, fac_ref, ord_ref, src_ref, slot_ref, scl_ref, mix_ref,
    wsem, ssem, rsem,
):
    d = lax.axis_index("dom")
    f = lax.axis_index("field")
    z = d // 16
    y = (d % 16) // 2
    k = d % 2

    def dom_at(step):
        return (d + step + ND) % ND

    def field_at(step):
        return (f + step) % NF

    pairs = (
        (tr_hbm, tr_ref), (dia_hbm, dia_ref), (fac_hbm, fac_ref), (ord_hbm, ord_ref), (src_hbm, src_ref),
        (ci_hbm, civ), (tb_hbm, tbv), (li_hbm, liv), (co_hbm, cov),
        (slot_hbm, slot_ref), (scl_hbm, scl_ref), (mix_hbm, mix_ref.at[f]),
    )
    fetch = [pltpu.make_async_copy(src, dst, wsem.at[i]) for i, (src, dst) in enumerate(pairs)]
    for c in fetch:
        c.start()

    field_peers = [(d, field_at(i)) for i in range(1, NF)]
    next_all = [(dom_at(1), field_at(i)) for i in range(NF)]
    prev_all = [(dom_at(-1), field_at(i)) for i in range(NF)]
    far = [(dom_at(2), f), (dom_at(-2), f)]
    z_peers = [(((z + i) % 8) * 16 + d % 16, f) for i in range(1, 8)]
    y_peers = [(z * 16 + ((y + i) % 8) * 2 + k, f) for i in range(1, 8)]
    core_peer = (d + 1 - 2 * k, f)
    greet = field_peers + next_all + prev_all + far + z_peers + y_peers
    barrier = pltpu.get_barrier_semaphore()
    for dev in greet:
        pl.semaphore_signal(barrier, inc=1, device_id=dev, device_id_type=MESH)

    count = [0]
    sent = []

    def send(src, dst, dev):
        n = count[0]
        count[0] += 1
        c = pltpu.make_async_remote_copy(
            src_ref=src, dst_ref=dst, send_sem=ssem.at[n], recv_sem=rsem.at[n],
            device_id=dev, device_id_type=MESH,
        )
        c.start()
        sent.append(c)
        return c

    pad16 = jnp.zeros((16, HE), BF)
    for g in range(NF):
        for h in range(2):
            lo_all[h, g, 176:192, :] = pad16

    own32[...] = jnp.zeros((CK, FACES), F32)
    fetch[0].wait()
    for c in range(2):
        own32[c * 32 : c * 32 + NFD, :] = tr_ref[:, c, :]
    ta[f, :, 0:FACES] = own32[...].astype(BF)
    rim1[0] = packed_rim(own32[:, 0:128], 0).astype(BF)
    rim1[1] = packed_rim(own32[:, 384:512], 96).astype(BF)
    pl.semaphore_wait(barrier, len(greet))

    ex1 = []
    for dev in next_all:
        ex1.append(send(rim1.at[1], xr1.at[0, f], dev))
    for dev in prev_all:
        ex1.append(send(rim1.at[0], xr1.at[1, f], dev))
    for dev in field_peers:
        ex1.append(send(ta.at[f, :, pl.ds(0, FACES)], ta.at[f, :, pl.ds(0, FACES)], dev))
    fetch[11].wait()
    exm = [send(mix_ref.at[f], mix_ref.at[f], dev) for dev in field_peers]
    fetch[1].wait()
    dia = jnp.concatenate([dia_ref[...]] * 4, axis=0)
    for zz in range(8):
        s1[zz] = pltpu.roll(dia, (8 - 64 * zz) % FACES, 1)[0:2, 0:128]
    dz = []
    for i in range(1, 8):
        dz.append(send(s1.at[(z + i) % 8], r1.at[z], z_peers[i - 1]))
    r1[z] = s1[z]

    rown = iota((256, 224), 0)
    rk = rown & 31
    want_r = jnp.where(rk < NFD, ((rown >> 5) & 1) * 112 + (rown >> 6) * NFD + rk, -1)
    permr = one_hot(iota((256, 224), 1) == want_r)
    colw = iota((672, 1024), 1)
    inn = colw & 255
    permw = one_hot(iota((672, 1024), 0) == jnp.where(inn < 168, (colw >> 8) * 168 + inn, -1))
    fetch[8].wait()
    wide = dot(dot(permr, cov[...]).astype(BF), permw).astype(BF)
    for g in range(NF):
        cop[g] = wide[:, g * 256 : (g + 1) * 256]
    half_rows = pl.ds(pl.multiple_of(k * 128, 128), 128)
    exw = []
    for i in range(1, NF):
        exw.append(send(cop.at[field_at(i), half_rows], cocol.at[f, half_rows], field_peers[i - 1]))
    cocol[f] = cop[f]

    fetch[2].wait()
    rel = (fac_ref[...] - d * FACES) & (ND * FACES - 1)
    lid = jnp.where(
        rel < FACES, rel, jnp.where(rel >= ND * FACES - RIM, rel - (ND * FACES - RIM) + FACES, rel + RIM)
    )
    for h in range(2):
        for j in range(4):
            c0 = h * 512 + j * HE
            oh[:, c0 : c0 + HE] = one_hot(iota((EXT, HE), 0) == lid[j : j + 1, h * HE : h * HE + HE])
    fetch[3].wait()
    order = ord_ref[...]
    face_n = (order + 1) * (order + 2)
    inner_n = face_n * (order + 3)
    face_live = 2 * (iota((256, ELEMS), 0) & 31) < face_n
    row = iota((2 * NID, ELEMS), 0)
    inner_live = 6 * jnp.where(row >= NID, row - NID, row) < inner_n
    fetch[4].wait()
    for c in range(2):
        srcf[c * NID : (c + 1) * NID, :] = src_ref[:, c, :].astype(F32)
    zero8 = jnp.zeros((8, HE), F32)

    col = iota((896, 1024), 1)
    kk = col & 31
    want = jnp.where(kk < NFD, ((col >> 5) & 7) * 112 + (col >> 8) * NFD + kk, -1)
    permk = one_hot(iota((896, 1024), 0) == want)
    fetch[5].wait()
    cip[...] = dot(civ[...], permk).astype(BF)
    fetch[6].wait()
    tbp[...] = dot(dot(permr, tbv[...]).astype(BF), permk).astype(BF)

    for c in ex1:
        c.wait_recv()
    for g in range(NF):
        ta[g, :, FACES:EXT] = (
            unpacked_rim(xr1[0, g].astype(F32), 0) + unpacked_rim(xr1[1, g].astype(F32), RIM)
        ).astype(BF)
    tall = ta[...].reshape(256, EXT)
    ex2 = [[], []]
    for h in range(2):
        es = slice(h * HE, h * HE + HE)
        picked = dot(tall, oh[:, h * 512 : h * 512 + 512])
        for j in range(4):
            live = jnp.where(face_live[:, es], picked[:, j * HE : (j + 1) * HE], 0.0)
            gat[h, j * 256 : (j + 1) * 256, :] = live.astype(BF)
        loads = srcf[:, es] - dot(cip[...], gat[h])
        loads = jnp.where(inner_live[:, es], loads, 0.0)
        lo_all[h, f, 0:176] = jnp.concatenate([loads, zero8], axis=0).astype(BF)
        for dev in field_peers:
            ex2[h].append(send(lo_all.at[h, f, pl.ds(0, 176)], lo_all.at[h, f, pl.ds(0, 176)], dev))
    for c in exm:
        c.wait_recv()
    for c in range(8):
        for c2 in range(8):
            coef = mix_ref[c // 2, c % 2 : c % 2 + 1, c2 : c2 + 1] + (1.0 if c == c2 else 0.0)
            cf[c * 8 + c2] = jnp.broadcast_to(coef, (8, 128))
    for c in exw:
        c.wait_recv()
    exf = []
    for i in range(1, NF):
        part = cocol.at[field_at(i), half_rows]
        exf.append(send(part, part, core_peer))
    for c in dz:
        c.wait_recv()
    for c in range(2):
        r2[y, c] = r1[:, c, :]
    dy = []
    for i in range(1, 8):
        dy.append(send(r2.at[y], r2.at[y], y_peers[i - 1]))

    colw = iota((672, PADK), 1)
    slab = (colw >= 192).astype(I32) + (colw >= 384).astype(I32) + (colw >= 576).astype(I32)
    inn = colw - slab * 192
    perms = one_hot(iota((672, PADK), 0) == jnp.where(inn < 168, slab * 168 + inn, -1))
    fetch[7].wait()
    lip[...] = dot(liv[...], perms).astype(BF)
    for h in range(2):
        tbg[h] = dot(tbp[...], gat[h])

    for c in exf:
        c.wait_recv()
    fetch[10].wait()
    zero88 = jnp.zeros((88, HE), F32)
    def mixed_share(part, c):
        total = None
        for c2 in range(8):
            coef = jnp.concatenate([cf[c * 8 + c2]] * 4, axis=0)
            coef = jnp.concatenate([coef] * (part.shape[1] // 128), axis=1)
            term = coef * part[c2 * 32 : c2 * 32 + 32]
            total = term if total is None else total + term
        return total

    flats = []
    for h in range(2):
        es = slice(h * HE, h * HE + HE)
        for c in ex2[h]:
            c.wait_recv()
        inter = dot(lip[...], lo_all[h].reshape(PADK, HE))
        inter = jnp.where(inner_live[:, es], inter, 0.0)
        inter = jnp.concatenate([inter, zero88], axis=0).astype(BF)
        his, los = [], []
        for g in range(NF):
            blocks = dot(cocol[g], inter) + jnp.where(f == g, tbg[h], 0.0)
            blocks = jnp.where(face_live[:, es], blocks, 0.0) * scl_ref[:, es]
            flat = jnp.concatenate([blocks[j * CK : (j + 1) * CK] for j in range(4)], axis=1)
            hi = flat.astype(BF)
            his.append(hi)
            los.append((flat - hi.astype(F32)).astype(BF))
        flats.append(jnp.concatenate(his + los, axis=0))
        if h == 0:
            rim_part = dot_nt(flats[0], oh[FACES:EXT, 0:512])
            acc_part = dot_nt(flats[0], oh[0:FACES, 0:512])

    rim_part = rim_part + dot_nt(flats[1], oh[FACES:EXT, 512:1024])
    rim_part = rim_part[0:256] + rim_part[256:512]
    for g in range(NF):
        rim = jnp.concatenate([mixed_share(rim_part, 2 * g), mixed_share(rim_part, 2 * g + 1)], axis=0)
        rim4[g, 0] = packed_rim(rim, 0).astype(BF)
        rim4[g, 1] = packed_rim(rim, RIM).astype(BF)

    ex4 = []
    for i in (2, 1, 3, 0):
        ex4.append(send(rim4.at[field_at(i), 0], xr4.at[0, f], prev_all[i]))
        ex4.append(send(rim4.at[field_at(i), 1], xr4.at[1, f], next_all[i]))
    acc_part = acc_part + dot_nt(flats[1], oh[0:FACES, 512:1024])
    acc_part = acc_part[0:256] + acc_part[256:512]
    for g in range(NF):
        own = jnp.concatenate([mixed_share(acc_part, 2 * g), mixed_share(acc_part, 2 * g + 1)], axis=0)
        mp[g] = own
        sb[g] = own.astype(BF)
    for i in (2, 1, 3):
        ex4.append(send(sb.at[field_at(i)], rb.at[f], field_peers[i - 1]))

    for c in dy:
        c.wait_recv()
    dk = send(r2, r3.at[k], core_peer)
    r3[k] = r2[...]

    fetch[9].wait()
    slots = slot_ref[...]
    parts = jnp.concatenate([(slots >> 4).astype(F32), (slots & 15).astype(F32)] + [jnp.zeros((6, FACES), F32)], axis=0)
    cs = iota((FACES, FACES), 1)
    spread = one_hot(iota((FACES, FACES), 0) == (cs & 127) * 4 + (cs >> 7))
    moved = dot(parts.astype(BF), spread).astype(I32)
    slot_qt = moved[0:1] * 16 + moved[1:2]
    pm[...] = one_hot(iota((FACES, FACES), 0) == slot_qt)

    dk.wait_recv()
    r_i = iota((128, 128), 0)
    t_of = (r_i & 7) * 16 + ((r_i >> 3) & 7) * 2 + (r_i >> 6)
    to_t = one_hot(iota((128, 128), 1) == t_of)
    for c in range(2):
        dt[c] = r3[:, :, c].reshape(128, 128).T
    start = 3 + 4 * (d % 16)
    lane = iota((1, 128), 1)
    for c in range(2):
        win = dt[c, pl.ds(start, 16), :]
        w0 = win.astype(BF)
        rest = win - w0.astype(F32)
        w1 = rest.astype(BF)
        w2 = (rest - w1.astype(F32)).astype(BF)
        got = dot(jnp.concatenate([w0, w1, w2], axis=0), to_t)
        dwin[c] = 1.0 / (got[0:16] + got[16:32] + got[32:48])

    def shifted(v, wrap, step):
        edge = 0 if step == 1 else 127
        rolled = jnp.where(lane == edge, 0.0, pltpu.roll(v, step % 128, 1))
        return jnp.where(wrap, rolled, v)

    wraps = [d <= 1] + [d == 0] * 4 + [None] * 4 + [d == ND - 1] * 4 + [d >= ND - 2]

    def placed(v, i):
        if i < 5:
            return shifted(v, wraps[i], 1)
        if i > 8:
            return shifted(v, wraps[i], -1)
        return v

    inv = []
    for c in range(2):
        inv.append([placed(jnp.broadcast_to(dwin[c, i : i + 1, :], (8, 128)), i) for i in range(14)])

    for c in ex4:
        c.wait_recv()

    both = mp[f]
    for i in range(1, NF):
        both = both + rb[field_at(i)].astype(F32)
    to_last = sum(xr4[0, g].astype(F32) for g in range(NF))
    to_first = sum(xr4[1, g].astype(F32) for g in range(NF))
    both = jnp.concatenate(
        [
            both[:, 0:128] + unpacked_rim(to_first, 0),
            both[:, 128:384],
            both[:, 384:512] + unpacked_rim(to_last, 96),
        ],
        axis=1,
    )
    moved_rhs = dot(hi_lo(both), pm[...])
    rhs = moved_rhs[0:CK] + moved_rhs[CK : 2 * CK]
    vb[...] = rhs.astype(BF)

    ex5 = [
        send(vb.at[:, pl.ds(384, 128)], ll, far[0]),
        send(vb.at[:, pl.ds(0, 128)], rr, far[1]),
        send(vb, ln, (dom_at(1), f)),
        send(vb, rn, (dom_at(-1), f)),
    ]
    for c in range(2):
        mixed_ref[c] = both[c * 32 : c * 32 + NFD]
    for c in ex5:
        c.wait_recv()

    corr = []
    for b in range(8):
        rows = slice(b * 8, b * 8 + 8)
        iv = inv[b // 4]
        pair = slice((b // 2) * 16, (b // 2) * 16 + 16)
        half = slice((b % 2) * 8, (b % 2) * 8 + 8)

        def get(ref, q):
            return ref[pair, q * 128 : (q + 1) * 128].astype(F32)[half]

        r = [get(ll, 0)] + [get(ln, q) for q in range(4)] + [rhs[rows, q * 128 : (q + 1) * 128] for q in range(4)]
        r = r + [get(rn, q) for q in range(4)] + [get(rr, 0)]
        yv = {i: iv[i] * placed(r[i], i) for i in range(14)}

        def residual(yy, zz, lo, hi):
            return {i: yy[i] + iv[i] * (zz[i - 1] + zz[i + 1]) - zz[i] for i in range(lo, hi)}

        def sweep(yy, lo, hi):
            step = dict(yy)
            total = dict(yy)
            rho = RHO0
            for _ in range(2):
                lo, hi = lo + 1, hi - 1
                rho_next = 1.0 / (2.0 * RATIO - rho)
                u = residual(yy, total, lo, hi)
                step = {i: (rho_next * rho) * step[i] + (2.0 * rho_next / HALF) * u[i] for i in range(lo, hi)}
                total = {i: total[i] + step[i] for i in range(lo, hi)}
                rho = rho_next
            return total, lo, hi

        first, lo, hi = sweep(yv, 0, 14)
        y2 = residual(yv, first, lo + 1, hi - 1)
        second, lo, hi = sweep(y2, lo + 1, hi - 1)
        corr.append(jnp.concatenate([first[i] + second[i] for i in range(5, 9)], axis=1))
    corr = jnp.concatenate(corr, axis=0)
    back = dot_nt(hi_lo(corr), pm[...])
    new = own32[...] - (back[0:CK] + back[CK : 2 * CK])
    for c in range(2):
        new_ref[c] = new[c * 32 : c * 32 + NFD]
    for c in sent:
        c.wait_send()


def turn(new_ref, mixed_ref, new_out, mixed_out):
    for c in range(2):
        new_out[:, c, :] = new_ref[c]
        mixed_out[:, c, :] = mixed_ref[c]


def shards(
    traces,
    interior_source,
    orders,
    element_scale,
    element_faces,
    solver_slots,
    line_diagonal,
    species_mix,
    couple_in,
    local_inverse,
    trace_block,
    couple_out,
):
    vmem = pl.BlockSpec(memory_space=pltpu.VMEM)
    hbm = pl.BlockSpec(memory_space=pltpu.HBM)
    n_copies = 64
    scratch = [
        pltpu.VMEM((NF, CK, EXT), BF),
        pltpu.VMEM((EXT, 1024), BF),
        pltpu.VMEM((2, 1024, HE), BF),
        pltpu.VMEM((168, 896), BF),
        pltpu.VMEM((168, 672), BF),
        pltpu.VMEM((224, 896), BF),
        pltpu.VMEM((224, 672), BF),
        pltpu.VMEM((168, 1024), BF),
        pltpu.VMEM((168, PADK), BF),
        pltpu.VMEM((256, 1024), BF),
        pltpu.VMEM((NF, 256, 256), BF),
        pltpu.VMEM((NF, 256, 256), BF),
        pltpu.VMEM((168, ELEMS), F32),
        pltpu.VMEM((2, NF, 192, HE), BF),
        pltpu.VMEM((NF, CK, FACES), F32),
        pltpu.VMEM((NF, CK, FACES), BF),
        pltpu.VMEM((NF, CK, FACES), BF),
        pltpu.VMEM((2, 16, 128), BF),
        pltpu.VMEM((2, NF, 16, 128), BF),
        pltpu.VMEM((NF, 2, 16, 128), BF),
        pltpu.VMEM((2, NF, 16, 128), BF),
        pltpu.VMEM((CK, FACES), BF),
        pltpu.VMEM((CK, FACES), BF),
        pltpu.VMEM((CK, FACES), BF),
        pltpu.VMEM((CK, 128), BF),
        pltpu.VMEM((CK, 128), BF),
        pltpu.VMEM((8, 2, 128), F32),
        pltpu.VMEM((8, 2, 128), F32),
        pltpu.VMEM((8, 2, 8, 128), F32),
        pltpu.VMEM((2, 8, 2, 8, 128), F32),
        pltpu.VMEM((2, 128, 128), F32),
        pltpu.VMEM((2, 16, 128), F32),
        pltpu.VMEM((FACES, FACES), BF),
        pltpu.VMEM((CK, FACES), F32),
        pltpu.VMEM((2, 256, HE), F32),
        pltpu.VMEM((64, 8, 128), F32),
        pltpu.VMEM((2, FACES), F32),
        pltpu.VMEM((NFD, 2, FACES), F32),
        pltpu.VMEM((4, ELEMS), I32),
        pltpu.VMEM((1, ELEMS), I32),
        pltpu.VMEM((NID, 2, ELEMS), BF),
        pltpu.VMEM((1, FACES), I32),
        pltpu.VMEM((1, ELEMS), F32),
        pltpu.VMEM((NF, 2, 8), F32),
        pltpu.SemaphoreType.DMA((12,)),
        pltpu.SemaphoreType.DMA((n_copies,)),
        pltpu.SemaphoreType.DMA((n_copies,)),
    ]
    shape = jax.ShapeDtypeStruct((2, NFD, FACES), F32)
    new, mixed = pl.pallas_call(
        kernel,
        out_shape=(shape, shape),
        in_specs=[hbm] * 12,
        out_specs=(vmem, vmem),
        scratch_shapes=scratch,
        compiler_params=pltpu.CompilerParams(
            collective_id=0, has_side_effects=True, vmem_limit_bytes=48 * 1024 * 1024
        ),
    )(
        pltpu.with_memory_space_constraint(line_diagonal, pltpu.HBM),
        pltpu.with_memory_space_constraint(jnp.transpose(traces, (1, 0, 2)), pltpu.HBM),
        pltpu.with_memory_space_constraint(element_faces, pltpu.HBM),
        pltpu.with_memory_space_constraint(orders.reshape(1, ELEMS), pltpu.HBM),
        pltpu.with_memory_space_constraint(jnp.transpose(interior_source, (1, 0, 2)), pltpu.HBM),
        pltpu.with_memory_space_constraint(couple_in, pltpu.HBM),
        pltpu.with_memory_space_constraint(trace_block, pltpu.HBM),
        pltpu.with_memory_space_constraint(local_inverse, pltpu.HBM),
        pltpu.with_memory_space_constraint(couple_out, pltpu.HBM),
        pltpu.with_memory_space_constraint(solver_slots.reshape(1, FACES), pltpu.HBM),
        pltpu.with_memory_space_constraint(element_scale.reshape(1, ELEMS), pltpu.HBM),
        pltpu.with_memory_space_constraint(species_mix, pltpu.HBM),
    )
    turned = jax.ShapeDtypeStruct((NFD, 2, FACES), F32)
    new, mixed = pl.pallas_call(
        turn,
        out_shape=(turned, turned),
        in_specs=[vmem] * 2,
        out_specs=(vmem, vmem),
        compiler_params=pltpu.CompilerParams(vmem_limit_bytes=4 * 1024 * 1024),
    )(new, mixed)
    return jnp.transpose(new, (1, 0, 2)), jnp.transpose(mixed, (1, 0, 2))


def solution(mesh):
    in_specs = (
        P("field", None, "dom"),
        P("field", None, "dom"),
        P("dom"),
        P("dom"),
        P(None, "dom"),
        P("dom"),
        P("field", "dom"),
        P("field", None),
        P("field", None),
        P("field", None),
        P("field", None),
        P("field", None),
    )
    out_specs = (P("field", None, "dom"), P("field", None, "dom"))
    return jax.shard_map(shards, mesh=mesh, in_specs=in_specs, out_specs=out_specs, check_vma=False)
```

```python
import functools

import jax
import jax.numpy as jnp
from jax import lax
from jax.experimental import pallas as pl
from jax.experimental.pallas import tpu as pltpu
from jax.sharding import PartitionSpec as P

F32 = jnp.float32
BF = jnp.bfloat16
I32 = jnp.int32
MESH = pl.DeviceIdType.MESH

NFD = 28
NID = 84
ND = 128
NF = 4
FACES = 512
ELEMS = 256
CK = 64
EXT = 640
PADK = 768
HE = 128
RIM = 32
RHO0 = 0.8
HALF = 0.8
RATIO = 1.25


def dot(a, b):
    return jnp.dot(a, b, preferred_element_type=F32)


def dot_nt(a, b):
    return lax.dot_general(a, b, (((1,), (1,)), ((), ())), preferred_element_type=F32)


def iota(shape, dim):
    return lax.broadcasted_iota(I32, shape, dim)


def one_hot(cond):
    return jnp.where(cond, 1.0, 0.0).astype(BF)


def hi_lo(x):
    hi = x.astype(BF)
    lo = (x - hi.astype(F32)).astype(BF)
    return jnp.concatenate([hi, lo], axis=0)


def packed_rim(x, lane0):
    lane = iota((16, 128), 1)
    out = jnp.zeros((16, 128), F32)
    for i in range(4):
        part = pltpu.roll(x[16 * i : 16 * i + 16], (RIM * i - lane0) % 128, 1)
        out = jnp.where((lane >= RIM * i) & (lane < RIM * i + RIM), part, out)
    return out


def unpacked_rim(x, lane0):
    lane = iota((16, 128), 1)
    keep = (lane >= lane0) & (lane < lane0 + RIM)
    parts = [jnp.where(keep, pltpu.roll(x, (lane0 - RIM * i) % 128, 1), 0.0) for i in range(4)]
    return jnp.concatenate(parts, axis=0)


def kernel(
    dia_hbm, tr_hbm, fac_hbm, ord_hbm, src_hbm, ci_hbm, tb_hbm, li_hbm, co_hbm, slot_hbm, scl_hbm, mix_hbm,
    new_ref, mixed_ref,
    ta, oh, gat, civ, liv, tbv, cov, cip, lip, tbp, cop, cocol, srcf,
    lo_all, mp, sb, rb, rim1, xr1, rim4, xr4, vb, ln, rn, ll, rr,
    s1, r1, r2, r3, dt, dwin, pm, own32, tbg, cf,
    dia_ref, tr_ref, fac_ref, ord_ref, src_ref, slot_ref, scl_ref, mix_ref,
    wsem, ssem, rsem,
):
    d = lax.axis_index("dom")
    f = lax.axis_index("field")
    z = d // 16
    y = (d % 16) // 2
    k = d % 2

    def dom_at(step):
        return (d + step + ND) % ND

    def field_at(step):
        return (f + step) % NF

    pairs = (
        (tr_hbm, tr_ref), (dia_hbm, dia_ref), (fac_hbm, fac_ref), (ord_hbm, ord_ref), (src_hbm, src_ref),
        (ci_hbm, civ), (tb_hbm, tbv), (li_hbm, liv), (co_hbm, cov),
        (slot_hbm, slot_ref), (scl_hbm, scl_ref), (mix_hbm, mix_ref.at[f]),
    )
    fetch = [pltpu.make_async_copy(src, dst, wsem.at[i]) for i, (src, dst) in enumerate(pairs)]
    for c in fetch:
        c.start()

    field_peers = [(d, field_at(i)) for i in range(1, NF)]
    far_first = [field_peers[1], field_peers[0], field_peers[2]]
    next_all = [(dom_at(1), field_at(i)) for i in range(NF)]
    prev_all = [(dom_at(-1), field_at(i)) for i in range(NF)]
    far = [(dom_at(2), f), (dom_at(-2), f)]
    z_peers = [(((z + i) % 8) * 16 + d % 16, f) for i in range(1, 8)]
    y_peers = [(z * 16 + ((y + i) % 8) * 2 + k, f) for i in range(1, 8)]
    core_peer = (d + 1 - 2 * k, f)
    greet = field_peers + next_all + prev_all + far + z_peers + y_peers
    barrier = pltpu.get_barrier_semaphore()
    for dev in greet:
        pl.semaphore_signal(barrier, inc=1, device_id=dev, device_id_type=MESH)

    count = [0]
    sent = []

    def send(src, dst, dev):
        n = count[0]
        count[0] += 1
        c = pltpu.make_async_remote_copy(
            src_ref=src, dst_ref=dst, send_sem=ssem.at[n], recv_sem=rsem.at[n],
            device_id=dev, device_id_type=MESH,
        )
        c.start()
        sent.append(c)
        return c

    pad16 = jnp.zeros((16, HE), BF)
    for g in range(NF):
        for h in range(2):
            lo_all[h, g, 176:192, :] = pad16

    own32[...] = jnp.zeros((CK, FACES), F32)
    fetch[0].wait()
    for c in range(2):
        own32[c * 32 : c * 32 + NFD, :] = tr_ref[:, c, :]
    ta[f, :, 0:FACES] = own32[...].astype(BF)
    rim1[0] = packed_rim(own32[:, 0:128], 0).astype(BF)
    rim1[1] = packed_rim(own32[:, 384:512], 96).astype(BF)
    pl.semaphore_wait(barrier, len(greet))

    ex1 = []
    for dev in next_all:
        ex1.append(send(rim1.at[1], xr1.at[0, f], dev))
    for dev in prev_all:
        ex1.append(send(rim1.at[0], xr1.at[1, f], dev))
    for dev in far_first:
        ex1.append(send(ta.at[f, :, pl.ds(0, FACES)], ta.at[f, :, pl.ds(0, FACES)], dev))
    fetch[11].wait()
    exm = [send(mix_ref.at[f], mix_ref.at[f], dev) for dev in field_peers]
    fetch[1].wait()
    dia = jnp.concatenate([dia_ref[...]] * 4, axis=0)
    for zz in range(8):
        s1[zz] = pltpu.roll(dia, (8 - 64 * zz) % FACES, 1)[0:2, 0:128]
    dz = []
    for i in range(1, 8):
        dz.append(send(s1.at[(z + i) % 8], r1.at[z], z_peers[i - 1]))
    r1[z] = s1[z]

    rown = iota((256, 224), 0)
    rk = rown & 31
    want_r = jnp.where(rk < NFD, ((rown >> 5) & 1) * 112 + (rown >> 6) * NFD + rk, -1)
    permr = one_hot(iota((256, 224), 1) == want_r)
    colw = iota((672, 1024), 1)
    inn = colw & 255
    permw = one_hot(iota((672, 1024), 0) == jnp.where(inn < 168, (colw >> 8) * 168 + inn, -1))
    fetch[8].wait()
    wide = dot(dot(permr, cov[...]).astype(BF), permw).astype(BF)
    for g in range(NF):
        cop[g] = wide[:, g * 256 : (g + 1) * 256]
    half_rows = pl.ds(pl.multiple_of(k * 128, 128), 128)
    exw = []
    for i in range(1, NF):
        exw.append(send(cop.at[field_at(i), half_rows], cocol.at[f, half_rows], field_peers[i - 1]))
    cocol[f] = cop[f]

    fetch[2].wait()
    rel = (fac_ref[...] - d * FACES) & (ND * FACES - 1)
    lid = jnp.where(
        rel < FACES, rel, jnp.where(rel >= ND * FACES - RIM, rel - (ND * FACES - RIM) + FACES, rel + RIM)
    )
    for h in range(2):
        for j in range(4):
            c0 = h * 512 + j * HE
            oh[:, c0 : c0 + HE] = one_hot(iota((EXT, HE), 0) == lid[j : j + 1, h * HE : h * HE + HE])
    fetch[3].wait()
    order = ord_ref[...]
    face_n = (order + 1) * (order + 2)
    inner_n = face_n * (order + 3)
    face_live = 2 * (iota((256, ELEMS), 0) & 31) < face_n
    row = iota((2 * NID, ELEMS), 0)
    inner_live = 6 * jnp.where(row >= NID, row - NID, row) < inner_n
    fetch[4].wait()
    for c in range(2):
        srcf[c * NID : (c + 1) * NID, :] = src_ref[:, c, :].astype(F32)
    zero8 = jnp.zeros((8, HE), F32)

    col = iota((896, 1024), 1)
    kk = col & 31
    want = jnp.where(kk < NFD, ((col >> 5) & 7) * 112 + (col >> 8) * NFD + kk, -1)
    permk = one_hot(iota((896, 1024), 0) == want)
    fetch[5].wait()
    cip[...] = dot(civ[...], permk).astype(BF)

    for c in ex1[0:8]:
        c.wait_recv()
    for g in range(NF):
        ta[g, :, FACES:EXT] = (
            unpacked_rim(xr1[0, g].astype(F32), 0) + unpacked_rim(xr1[1, g].astype(F32), RIM)
        ).astype(BF)
    for c in ex1[8:]:
        c.wait_recv()
    tall = ta[...].reshape(256, EXT)
    ex2 = [[], []]
    for h in range(2):
        es = slice(h * HE, h * HE + HE)
        picked = dot(tall, oh[:, h * 512 : h * 512 + 512])
        for j in range(4):
            live = jnp.where(face_live[:, es], picked[:, j * HE : (j + 1) * HE], 0.0)
            gat[h, j * 256 : (j + 1) * 256, :] = live.astype(BF)
        loads = srcf[:, es] - dot(cip[...], gat[h])
        loads = jnp.where(inner_live[:, es], loads, 0.0)
        lo_all[h, f, 0:176] = jnp.concatenate([loads, zero8], axis=0).astype(BF)
        for dev in far_first:
            ex2[h].append(send(lo_all.at[h, f, pl.ds(0, 176)], lo_all.at[h, f, pl.ds(0, 176)], dev))
    for c in exm:
        c.wait_recv()
    for c in range(8):
        for c2 in range(8):
            coef = mix_ref[c // 2, c % 2 : c % 2 + 1, c2 : c2 + 1] + (1.0 if c == c2 else 0.0)
            cf[c * 8 + c2] = jnp.broadcast_to(coef, (8, 128))
    for c in exw:
        c.wait_recv()
    exf = []
    for i in range(1, NF):
        part = cocol.at[field_at(i), half_rows]
        exf.append(send(part, part, core_peer))
    for c in dz:
        c.wait_recv()
    for c in range(2):
        r2[y, c] = r1[:, c, :]
    dy = []
    for i in range(1, 8):
        dy.append(send(r2.at[y], r2.at[y], y_peers[i - 1]))

    colw = iota((672, PADK), 1)
    slab = (colw >= 192).astype(I32) + (colw >= 384).astype(I32) + (colw >= 576).astype(I32)
    inn = colw - slab * 192
    perms = one_hot(iota((672, PADK), 0) == jnp.where(inn < 168, slab * 168 + inn, -1))
    fetch[7].wait()
    lip[...] = dot(liv[...], perms).astype(BF)
    fetch[6].wait()
    tbp[...] = dot(dot(permr, tbv[...]).astype(BF), permk).astype(BF)
    for h in range(2):
        tbg[h] = dot(tbp[...], gat[h])

    for c in exf:
        c.wait_recv()
    fetch[10].wait()
    zero88 = jnp.zeros((88, HE), F32)
    def mixed_share(part, c):
        total = None
        for c2 in range(8):
            coef = jnp.concatenate([cf[c * 8 + c2]] * 4, axis=0)
            coef = jnp.concatenate([coef] * (part.shape[1] // 128), axis=1)
            term = coef * part[c2 * 32 : c2 * 32 + 32]
            total = term if total is None else total + term
        return total

    flats = []
    for h in range(2):
        es = slice(h * HE, h * HE + HE)
        for c in ex2[h]:
            c.wait_recv()
        inter = dot(lip[...], lo_all[h].reshape(PADK, HE))
        inter = jnp.where(inner_live[:, es], inter, 0.0)
        inter = jnp.concatenate([inter, zero88], axis=0).astype(BF)
        his, los = [], []
        for g in range(NF):
            blocks = dot(cocol[g], inter) + jnp.where(f == g, tbg[h], 0.0)
            blocks = jnp.where(face_live[:, es], blocks, 0.0) * scl_ref[:, es]
            flat = jnp.concatenate([blocks[j * CK : (j + 1) * CK] for j in range(4)], axis=1)
            hi = flat.astype(BF)
            his.append(hi)
            los.append((flat - hi.astype(F32)).astype(BF))
        flats.append(jnp.concatenate(his + los, axis=0))
        if h == 0:
            rim_part = dot_nt(flats[0], oh[FACES:EXT, 0:512])
            acc_part = dot_nt(flats[0], oh[0:FACES, 0:512])

    rim_part = rim_part + dot_nt(flats[1], oh[FACES:EXT, 512:1024])
    rim_part = rim_part[0:256] + rim_part[256:512]
    for g in range(NF):
        rim = jnp.concatenate([mixed_share(rim_part, 2 * g), mixed_share(rim_part, 2 * g + 1)], axis=0)
        rim4[g, 0] = packed_rim(rim, 0).astype(BF)
        rim4[g, 1] = packed_rim(rim, RIM).astype(BF)

    ex4 = []
    for i in (2, 1, 3, 0):
        ex4.append(send(rim4.at[field_at(i), 0], xr4.at[0, f], prev_all[i]))
        ex4.append(send(rim4.at[field_at(i), 1], xr4.at[1, f], next_all[i]))
    acc_part = acc_part + dot_nt(flats[1], oh[0:FACES, 512:1024])
    acc_part = acc_part[0:256] + acc_part[256:512]
    for g in range(NF):
        own = jnp.concatenate([mixed_share(acc_part, 2 * g), mixed_share(acc_part, 2 * g + 1)], axis=0)
        mp[g] = own
        sb[g] = own.astype(BF)
    for i in (2, 1, 3):
        ex4.append(send(sb.at[field_at(i)], rb.at[f], field_peers[i - 1]))

    for c in dy:
        c.wait_recv()
    dk = send(r2, r3.at[k], core_peer)
    r3[k] = r2[...]

    fetch[9].wait()
    slots = slot_ref[...]
    parts = jnp.concatenate([(slots >> 4).astype(F32), (slots & 15).astype(F32)] + [jnp.zeros((6, FACES), F32)], axis=0)
    cs = iota((FACES, FACES), 1)
    spread = one_hot(iota((FACES, FACES), 0) == (cs & 127) * 4 + (cs >> 7))
    moved = dot(parts.astype(BF), spread).astype(I32)
    slot_qt = moved[0:1] * 16 + moved[1:2]
    pm[...] = one_hot(iota((FACES, FACES), 0) == slot_qt)

    dk.wait_recv()
    r_i = iota((128, 128), 0)
    t_of = (r_i & 7) * 16 + ((r_i >> 3) & 7) * 2 + (r_i >> 6)
    to_t = one_hot(iota((128, 128), 1) == t_of)
    for c in range(2):
        dt[c] = r3[:, :, c].reshape(128, 128).T
    start = 3 + 4 * (d % 16)
    lane = iota((1, 128), 1)
    for c in range(2):
        win = dt[c, pl.ds(start, 16), :]
        w0 = win.astype(BF)
        rest = win - w0.astype(F32)
        w1 = rest.astype(BF)
        w2 = (rest - w1.astype(F32)).astype(BF)
        got = dot(jnp.concatenate([w0, w1, w2], axis=0), to_t)
        dwin[c] = 1.0 / (got[0:16] + got[16:32] + got[32:48])

    def shifted(v, wrap, step):
        edge = 0 if step == 1 else 127
        rolled = jnp.where(lane == edge, 0.0, pltpu.roll(v, step % 128, 1))
        return jnp.where(wrap, rolled, v)

    wraps = [d <= 1] + [d == 0] * 4 + [None] * 4 + [d == ND - 1] * 4 + [d >= ND - 2]

    def placed(v, i):
        if i < 5:
            return shifted(v, wraps[i], 1)
        if i > 8:
            return shifted(v, wraps[i], -1)
        return v

    inv = []
    for c in range(2):
        inv.append([placed(jnp.broadcast_to(dwin[c, i : i + 1, :], (8, 128)), i) for i in range(14)])

    for c in ex4:
        c.wait_recv()

    both = mp[f]
    for i in range(1, NF):
        both = both + rb[field_at(i)].astype(F32)
    to_last = sum(xr4[0, g].astype(F32) for g in range(NF))
    to_first = sum(xr4[1, g].astype(F32) for g in range(NF))
    both = jnp.concatenate(
        [
            both[:, 0:128] + unpacked_rim(to_first, 0),
            both[:, 128:384],
            both[:, 384:512] + unpacked_rim(to_last, 96),
        ],
        axis=1,
    )
    moved_rhs = dot(hi_lo(both), pm[...])
    rhs = moved_rhs[0:CK] + moved_rhs[CK : 2 * CK]
    vb[...] = rhs.astype(BF)

    ex5 = [
        send(vb.at[:, pl.ds(384, 128)], ll, far[0]),
        send(vb.at[:, pl.ds(0, 128)], rr, far[1]),
        send(vb, ln, (dom_at(1), f)),
        send(vb, rn, (dom_at(-1), f)),
    ]
    for c in sent[:-4]:
        c.wait_send()
    for c in range(2):
        mixed_ref[c] = both[c * 32 : c * 32 + NFD]
    for c in ex5:
        c.wait_recv()

    corr = []
    for b in range(8):
        rows = slice(b * 8, b * 8 + 8)
        iv = inv[b // 4]
        pair = slice((b // 2) * 16, (b // 2) * 16 + 16)
        half = slice((b % 2) * 8, (b % 2) * 8 + 8)

        def get(ref, q):
            return ref[pair, q * 128 : (q + 1) * 128].astype(F32)[half]

        r = [get(ll, 0)] + [get(ln, q) for q in range(4)] + [rhs[rows, q * 128 : (q + 1) * 128] for q in range(4)]
        r = r + [get(rn, q) for q in range(4)] + [get(rr, 0)]
        yv = {i: iv[i] * placed(r[i], i) for i in range(14)}

        def residual(yy, zz, lo, hi):
            return {i: yy[i] + iv[i] * (zz[i - 1] + zz[i + 1]) - zz[i] for i in range(lo, hi)}

        def sweep(yy, lo, hi):
            step = dict(yy)
            total = dict(yy)
            rho = RHO0
            for _ in range(2):
                lo, hi = lo + 1, hi - 1
                rho_next = 1.0 / (2.0 * RATIO - rho)
                u = residual(yy, total, lo, hi)
                step = {i: (rho_next * rho) * step[i] + (2.0 * rho_next / HALF) * u[i] for i in range(lo, hi)}
                total = {i: total[i] + step[i] for i in range(lo, hi)}
                rho = rho_next
            return total, lo, hi

        first, lo, hi = sweep(yv, 0, 14)
        y2 = residual(yv, first, lo + 1, hi - 1)
        second, lo, hi = sweep(y2, lo + 1, hi - 1)
        corr.append(jnp.concatenate([first[i] + second[i] for i in range(5, 9)], axis=1))
    corr = jnp.concatenate(corr, axis=0)
    back = dot_nt(hi_lo(corr), pm[...])
    new = own32[...] - (back[0:CK] + back[CK : 2 * CK])
    for c in range(2):
        new_ref[c] = new[c * 32 : c * 32 + NFD]
    for c in ex5:
        c.wait_send()


def turn(new_ref, mixed_ref, new_out, mixed_out):
    for c in range(2):
        new_out[:, c, :] = new_ref[c]
        mixed_out[:, c, :] = mixed_ref[c]


def shards(
    traces,
    interior_source,
    orders,
    element_scale,
    element_faces,
    solver_slots,
    line_diagonal,
    species_mix,
    couple_in,
    local_inverse,
    trace_block,
    couple_out,
):
    vmem = pl.BlockSpec(memory_space=pltpu.VMEM)
    hbm = pl.BlockSpec(memory_space=pltpu.HBM)
    n_copies = 64
    scratch = [
        pltpu.VMEM((NF, CK, EXT), BF),
        pltpu.VMEM((EXT, 1024), BF),
        pltpu.VMEM((2, 1024, HE), BF),
        pltpu.VMEM((168, 896), BF),
        pltpu.VMEM((168, 672), BF),
        pltpu.VMEM((224, 896), BF),
        pltpu.VMEM((224, 672), BF),
        pltpu.VMEM((168, 1024), BF),
        pltpu.VMEM((168, PADK), BF),
        pltpu.VMEM((256, 1024), BF),
        pltpu.VMEM((NF, 256, 256), BF),
        pltpu.VMEM((NF, 256, 256), BF),
        pltpu.VMEM((168, ELEMS), F32),
        pltpu.VMEM((2, NF, 192, HE), BF),
        pltpu.VMEM((NF, CK, FACES), F32),
        pltpu.VMEM((NF, CK, FACES), BF),
        pltpu.VMEM((NF, CK, FACES), BF),
        pltpu.VMEM((2, 16, 128), BF),
        pltpu.VMEM((2, NF, 16, 128), BF),
        pltpu.VMEM((NF, 2, 16, 128), BF),
        pltpu.VMEM((2, NF, 16, 128), BF),
        pltpu.VMEM((CK, FACES), BF),
        pltpu.VMEM((CK, FACES), BF),
        pltpu.VMEM((CK, FACES), BF),
        pltpu.VMEM((CK, 128), BF),
        pltpu.VMEM((CK, 128), BF),
        pltpu.VMEM((8, 2, 128), F32),
        pltpu.VMEM((8, 2, 128), F32),
        pltpu.VMEM((8, 2, 8, 128), F32),
        pltpu.VMEM((2, 8, 2, 8, 128), F32),
        pltpu.VMEM((2, 128, 128), F32),
        pltpu.VMEM((2, 16, 128), F32),
        pltpu.VMEM((FACES, FACES), BF),
        pltpu.VMEM((CK, FACES), F32),
        pltpu.VMEM((2, 256, HE), F32),
        pltpu.VMEM((64, 8, 128), F32),
        pltpu.VMEM((2, FACES), F32),
        pltpu.VMEM((NFD, 2, FACES), F32),
        pltpu.VMEM((4, ELEMS), I32),
        pltpu.VMEM((1, ELEMS), I32),
        pltpu.VMEM((NID, 2, ELEMS), BF),
        pltpu.VMEM((1, FACES), I32),
        pltpu.VMEM((1, ELEMS), F32),
        pltpu.VMEM((NF, 2, 8), F32),
        pltpu.SemaphoreType.DMA((12,)),
        pltpu.SemaphoreType.DMA((n_copies,)),
        pltpu.SemaphoreType.DMA((n_copies,)),
    ]
    shape = jax.ShapeDtypeStruct((2, NFD, FACES), F32)
    new, mixed = pl.pallas_call(
        kernel,
        out_shape=(shape, shape),
        in_specs=[hbm] * 12,
        out_specs=(vmem, vmem),
        scratch_shapes=scratch,
        compiler_params=pltpu.CompilerParams(
            collective_id=0, has_side_effects=True, vmem_limit_bytes=48 * 1024 * 1024
        ),
    )(
        pltpu.with_memory_space_constraint(line_diagonal, pltpu.HBM),
        pltpu.with_memory_space_constraint(jnp.transpose(traces, (1, 0, 2)), pltpu.HBM),
        pltpu.with_memory_space_constraint(element_faces, pltpu.HBM),
        pltpu.with_memory_space_constraint(orders.reshape(1, ELEMS), pltpu.HBM),
        pltpu.with_memory_space_constraint(jnp.transpose(interior_source, (1, 0, 2)), pltpu.HBM),
        pltpu.with_memory_space_constraint(couple_in, pltpu.HBM),
        pltpu.with_memory_space_constraint(trace_block, pltpu.HBM),
        pltpu.with_memory_space_constraint(local_inverse, pltpu.HBM),
        pltpu.with_memory_space_constraint(couple_out, pltpu.HBM),
        pltpu.with_memory_space_constraint(solver_slots.reshape(1, FACES), pltpu.HBM),
        pltpu.with_memory_space_constraint(element_scale.reshape(1, ELEMS), pltpu.HBM),
        pltpu.with_memory_space_constraint(species_mix, pltpu.HBM),
    )
    turned = jax.ShapeDtypeStruct((NFD, 2, FACES), F32)
    new, mixed = pl.pallas_call(
        turn,
        out_shape=(turned, turned),
        in_specs=[vmem] * 2,
        out_specs=(vmem, vmem),
        compiler_params=pltpu.CompilerParams(vmem_limit_bytes=4 * 1024 * 1024),
    )(new, mixed)
    return jnp.transpose(new, (1, 0, 2)), jnp.transpose(mixed, (1, 0, 2))


def solution(mesh):
    in_specs = (
        P("field", None, "dom"),
        P("field", None, "dom"),
        P("dom"),
        P("dom"),
        P(None, "dom"),
        P("dom"),
        P("field", "dom"),
        P("field", None),
        P("field", None),
        P("field", None),
        P("field", None),
        P("field", None),
    )
    out_specs = (P("field", None, "dom"), P("field", None, "dom"))
    return jax.shard_map(shards, mesh=mesh, in_specs=in_specs, out_specs=out_specs, check_vma=False)
```

```python
import functools

import jax
import jax.numpy as jnp
from jax import lax
from jax.experimental import pallas as pl
from jax.experimental.pallas import tpu as pltpu
from jax.sharding import PartitionSpec as P

F32 = jnp.float32
BF = jnp.bfloat16
I32 = jnp.int32
MESH = pl.DeviceIdType.MESH

NFD = 28
NID = 84
ND = 128
NF = 4
FACES = 512
ELEMS = 256
CK = 64
EXT = 640
PADK = 768
HE = 128
RIM = 32
RHO0 = 0.8
HALF = 0.8
RATIO = 1.25


def dot(a, b):
    return jnp.dot(a, b, preferred_element_type=F32)


def dot_nt(a, b):
    return lax.dot_general(a, b, (((1,), (1,)), ((), ())), preferred_element_type=F32)


def iota(shape, dim):
    return lax.broadcasted_iota(I32, shape, dim)


def one_hot(cond):
    return jnp.where(cond, 1.0, 0.0).astype(BF)


def hi_lo(x):
    hi = x.astype(BF)
    lo = (x - hi.astype(F32)).astype(BF)
    return jnp.concatenate([hi, lo], axis=0)


def packed_rim(x, lane0):
    lane = iota((16, 128), 1)
    out = jnp.zeros((16, 128), F32)
    for i in range(4):
        part = pltpu.roll(x[16 * i : 16 * i + 16], (RIM * i - lane0) % 128, 1)
        out = jnp.where((lane >= RIM * i) & (lane < RIM * i + RIM), part, out)
    return out


def unpacked_rim(x, lane0):
    lane = iota((16, 128), 1)
    keep = (lane >= lane0) & (lane < lane0 + RIM)
    parts = [jnp.where(keep, pltpu.roll(x, (lane0 - RIM * i) % 128, 1), 0.0) for i in range(4)]
    return jnp.concatenate(parts, axis=0)


def kernel(
    dia_hbm, tr_hbm, fac_hbm, ord_hbm, src_hbm, ci_hbm, tb_hbm, li_hbm, co_hbm, slot_hbm, scl_hbm, mix_hbm,
    new_ref, mixed_ref,
    ta, oh, gat, civ, liv, tbv, cov, cip, lip, tbp, cop, cocol, srcf,
    lo_all, mp, sb, rb, rim1, xr1, rim4, xr4, vb, ln, rn, ll, rr,
    s1, r1, r2, r3, dt, dwin, pm, own32, tbg, cf,
    dia_ref, tr_ref, fac_ref, ord_ref, src_ref, slot_ref, scl_ref, mix_ref,
    wsem, ssem, rsem,
):
    d = lax.axis_index("dom")
    f = lax.axis_index("field")
    z = d // 16
    y = (d % 16) // 2
    k = d % 2

    def dom_at(step):
        return (d + step + ND) % ND

    def field_at(step):
        return (f + step) % NF

    pairs = (
        (tr_hbm, tr_ref), (dia_hbm, dia_ref), (fac_hbm, fac_ref), (ord_hbm, ord_ref), (src_hbm, src_ref),
        (ci_hbm, civ), (tb_hbm, tbv), (li_hbm, liv), (co_hbm, cov),
        (slot_hbm, slot_ref), (scl_hbm, scl_ref), (mix_hbm, mix_ref.at[f]),
    )
    fetch = [pltpu.make_async_copy(src, dst, wsem.at[i]) for i, (src, dst) in enumerate(pairs)]
    fetch[0].start()

    field_peers = [(d, field_at(i)) for i in range(1, NF)]
    far_first = [field_peers[1], field_peers[0], field_peers[2]]
    next_all = [(dom_at(1), field_at(i)) for i in range(NF)]
    prev_all = [(dom_at(-1), field_at(i)) for i in range(NF)]
    far = [(dom_at(2), f), (dom_at(-2), f)]
    z_peers = [(((z + i) % 8) * 16 + d % 16, f) for i in range(1, 8)]
    y_peers = [(z * 16 + ((y + i) % 8) * 2 + k, f) for i in range(1, 8)]
    core_peer = (d + 1 - 2 * k, f)
    hops = [side[i] for i in (2, 1, 3, 0) for side in (next_all, prev_all)]
    greet = hops + far_first + far + z_peers + y_peers
    barrier = pltpu.get_barrier_semaphore()
    for dev in greet:
        pl.semaphore_signal(barrier, inc=1, device_id=dev, device_id_type=MESH)
    for c in fetch[1:]:
        c.start()

    count = [0]
    sent = []

    def send(src, dst, dev):
        n = count[0]
        count[0] += 1
        c = pltpu.make_async_remote_copy(
            src_ref=src, dst_ref=dst, send_sem=ssem.at[n], recv_sem=rsem.at[n],
            device_id=dev, device_id_type=MESH,
        )
        c.start()
        sent.append(c)
        return c

    pad16 = jnp.zeros((16, HE), BF)
    for g in range(NF):
        for h in range(2):
            lo_all[h, g, 176:192, :] = pad16

    own32[...] = jnp.zeros((CK, FACES), F32)
    fetch[0].wait()
    for c in range(2):
        own32[c * 32 : c * 32 + NFD, :] = tr_ref[:, c, :]
    ta[f, :, 0:FACES] = own32[...].astype(BF)
    rim1[0] = packed_rim(own32[:, 0:128], 0).astype(BF)
    rim1[1] = packed_rim(own32[:, 384:512], 96).astype(BF)
    pl.semaphore_wait(barrier, len(greet))

    ex1 = []
    for dev in next_all:
        ex1.append(send(rim1.at[1], xr1.at[0, f], dev))
    for dev in prev_all:
        ex1.append(send(rim1.at[0], xr1.at[1, f], dev))
    for dev in far_first:
        ex1.append(send(ta.at[f, :, pl.ds(0, FACES)], ta.at[f, :, pl.ds(0, FACES)], dev))
    fetch[11].wait()
    exm = [send(mix_ref.at[f], mix_ref.at[f], dev) for dev in field_peers]
    fetch[1].wait()
    dia = jnp.concatenate([dia_ref[...]] * 4, axis=0)
    for zz in range(8):
        s1[zz] = pltpu.roll(dia, (8 - 64 * zz) % FACES, 1)[0:2, 0:128]
    dz = []
    for i in range(1, 8):
        dz.append(send(s1.at[(z + i) % 8], r1.at[z], z_peers[i - 1]))
    r1[z] = s1[z]

    rown = iota((256, 224), 0)
    rk = rown & 31
    want_r = jnp.where(rk < NFD, ((rown >> 5) & 1) * 112 + (rown >> 6) * NFD + rk, -1)
    permr = one_hot(iota((256, 224), 1) == want_r)
    colw = iota((672, 1024), 1)
    inn = colw & 255
    permw = one_hot(iota((672, 1024), 0) == jnp.where(inn < 168, (colw >> 8) * 168 + inn, -1))
    fetch[8].wait()
    wide = dot(dot(permr, cov[...]).astype(BF), permw).astype(BF)
    for g in range(NF):
        cop[g] = wide[:, g * 256 : (g + 1) * 256]
    half_rows = pl.ds(pl.multiple_of(k * 128, 128), 128)
    exw = []
    for i in range(1, NF):
        exw.append(send(cop.at[field_at(i), half_rows], cocol.at[f, half_rows], field_peers[i - 1]))
    cocol[f] = cop[f]

    fetch[2].wait()
    rel = (fac_ref[...] - d * FACES) & (ND * FACES - 1)
    lid = jnp.where(
        rel < FACES, rel, jnp.where(rel >= ND * FACES - RIM, rel - (ND * FACES - RIM) + FACES, rel + RIM)
    )
    for h in range(2):
        for j in range(4):
            c0 = h * 512 + j * HE
            oh[:, c0 : c0 + HE] = one_hot(iota((EXT, HE), 0) == lid[j : j + 1, h * HE : h * HE + HE])
    fetch[3].wait()
    order = ord_ref[...]
    face_n = (order + 1) * (order + 2)
    inner_n = face_n * (order + 3)
    face_live = 2 * (iota((256, ELEMS), 0) & 31) < face_n
    row = iota((2 * NID, ELEMS), 0)
    inner_live = 6 * jnp.where(row >= NID, row - NID, row) < inner_n
    fetch[4].wait()
    for c in range(2):
        srcf[c * NID : (c + 1) * NID, :] = src_ref[:, c, :].astype(F32)
    zero8 = jnp.zeros((8, HE), F32)

    col = iota((896, 1024), 1)
    kk = col & 31
    want = jnp.where(kk < NFD, ((col >> 5) & 7) * 112 + (col >> 8) * NFD + kk, -1)
    permk = one_hot(iota((896, 1024), 0) == want)
    fetch[5].wait()
    cip[...] = dot(civ[...], permk).astype(BF)

    for c in ex1[0:8]:
        c.wait_recv()
    for g in range(NF):
        ta[g, :, FACES:EXT] = (
            unpacked_rim(xr1[0, g].astype(F32), 0) + unpacked_rim(xr1[1, g].astype(F32), RIM)
        ).astype(BF)
    for c in ex1[8:]:
        c.wait_recv()
    tall = ta[...].reshape(256, EXT)
    ex2 = [[], []]
    for h in range(2):
        es = slice(h * HE, h * HE + HE)
        picked = dot(tall, oh[:, h * 512 : h * 512 + 512])
        for j in range(4):
            live = jnp.where(face_live[:, es], picked[:, j * HE : (j + 1) * HE], 0.0)
            gat[h, j * 256 : (j + 1) * 256, :] = live.astype(BF)
        loads = srcf[:, es] - dot(cip[...], gat[h])
        loads = jnp.where(inner_live[:, es], loads, 0.0)
        lo_all[h, f, 0:176] = jnp.concatenate([loads, zero8], axis=0).astype(BF)
        for dev in far_first:
            ex2[h].append(send(lo_all.at[h, f, pl.ds(0, 176)], lo_all.at[h, f, pl.ds(0, 176)], dev))
    for c in exm:
        c.wait_recv()
    for c in range(8):
        for c2 in range(8):
            coef = mix_ref[c // 2, c % 2 : c % 2 + 1, c2 : c2 + 1] + (1.0 if c == c2 else 0.0)
            cf[c * 8 + c2] = jnp.broadcast_to(coef, (8, 128))
    for c in exw:
        c.wait_recv()
    exf = []
    for i in range(1, NF):
        part = cocol.at[field_at(i), half_rows]
        exf.append(send(part, part, core_peer))
    for c in dz:
        c.wait_recv()
    for c in range(2):
        r2[y, c] = r1[:, c, :]
    dy = []
    for i in range(1, 8):
        dy.append(send(r2.at[y], r2.at[y], y_peers[i - 1]))

    colw = iota((672, PADK), 1)
    slab = (colw >= 192).astype(I32) + (colw >= 384).astype(I32) + (colw >= 576).astype(I32)
    inn = colw - slab * 192
    perms = one_hot(iota((672, PADK), 0) == jnp.where(inn < 168, slab * 168 + inn, -1))
    fetch[7].wait()
    lip[...] = dot(liv[...], perms).astype(BF)
    fetch[6].wait()
    tbp[...] = dot(dot(permr, tbv[...]).astype(BF), permk).astype(BF)
    for h in range(2):
        tbg[h] = dot(tbp[...], gat[h])

    for c in exf:
        c.wait_recv()
    fetch[10].wait()
    zero88 = jnp.zeros((88, HE), F32)
    def mixed_share(part, c):
        total = None
        for c2 in range(8):
            coef = jnp.concatenate([cf[c * 8 + c2]] * 4, axis=0)
            coef = jnp.concatenate([coef] * (part.shape[1] // 128), axis=1)
            term = coef * part[c2 * 32 : c2 * 32 + 32]
            total = term if total is None else total + term
        return total

    flats = []
    for h in range(2):
        es = slice(h * HE, h * HE + HE)
        for c in ex2[h]:
            c.wait_recv()
        inter = dot(lip[...], lo_all[h].reshape(PADK, HE))
        inter = jnp.where(inner_live[:, es], inter, 0.0)
        inter = jnp.concatenate([inter, zero88], axis=0).astype(BF)
        his, los = [], []
        for g in range(NF):
            blocks = dot(cocol[g], inter) + jnp.where(f == g, tbg[h], 0.0)
            blocks = jnp.where(face_live[:, es], blocks, 0.0) * scl_ref[:, es]
            flat = jnp.concatenate([blocks[j * CK : (j + 1) * CK] for j in range(4)], axis=1)
            hi = flat.astype(BF)
            his.append(hi)
            los.append((flat - hi.astype(F32)).astype(BF))
        flats.append(jnp.concatenate(his + los, axis=0))
        if h == 0:
            rim_part = dot_nt(flats[0], oh[FACES:EXT, 0:512])
            acc_part = dot_nt(flats[0], oh[0:FACES, 0:512])

    rim_part = rim_part + dot_nt(flats[1], oh[FACES:EXT, 512:1024])
    rim_part = rim_part[0:256] + rim_part[256:512]
    for g in range(NF):
        rim = jnp.concatenate([mixed_share(rim_part, 2 * g), mixed_share(rim_part, 2 * g + 1)], axis=0)
        rim4[g, 0] = packed_rim(rim, 0).astype(BF)
        rim4[g, 1] = packed_rim(rim, RIM).astype(BF)

    ex4 = []
    for i in (2, 1, 3, 0):
        ex4.append(send(rim4.at[field_at(i), 0], xr4.at[0, f], prev_all[i]))
        ex4.append(send(rim4.at[field_at(i), 1], xr4.at[1, f], next_all[i]))
    acc_part = acc_part + dot_nt(flats[1], oh[0:FACES, 512:1024])
    acc_part = acc_part[0:256] + acc_part[256:512]
    for g in range(NF):
        own = jnp.concatenate([mixed_share(acc_part, 2 * g), mixed_share(acc_part, 2 * g + 1)], axis=0)
        mp[g] = own
        sb[g] = own.astype(BF)
    for i in (2, 1, 3):
        ex4.append(send(sb.at[field_at(i)], rb.at[f], field_peers[i - 1]))

    for c in dy:
        c.wait_recv()
    dk = send(r2, r3.at[k], core_peer)
    r3[k] = r2[...]

    fetch[9].wait()
    slots = slot_ref[...]
    parts = jnp.concatenate([(slots >> 4).astype(F32), (slots & 15).astype(F32)] + [jnp.zeros((6, FACES), F32)], axis=0)
    cs = iota((FACES, FACES), 1)
    spread = one_hot(iota((FACES, FACES), 0) == (cs & 127) * 4 + (cs >> 7))
    moved = dot(parts.astype(BF), spread).astype(I32)
    slot_qt = moved[0:1] * 16 + moved[1:2]
    pm[...] = one_hot(iota((FACES, FACES), 0) == slot_qt)

    dk.wait_recv()
    r_i = iota((128, 128), 0)
    t_of = (r_i & 7) * 16 + ((r_i >> 3) & 7) * 2 + (r_i >> 6)
    to_t = one_hot(iota((128, 128), 1) == t_of)
    for c in range(2):
        dt[c] = r3[:, :, c].reshape(128, 128).T
    start = 3 + 4 * (d % 16)
    lane = iota((1, 128), 1)
    for c in range(2):
        win = dt[c, pl.ds(start, 16), :]
        w0 = win.astype(BF)
        rest = win - w0.astype(F32)
        w1 = rest.astype(BF)
        w2 = (rest - w1.astype(F32)).astype(BF)
        got = dot(jnp.concatenate([w0, w1, w2], axis=0), to_t)
        dwin[c] = 1.0 / (got[0:16] + got[16:32] + got[32:48])

    def shifted(v, wrap, step):
        edge = 0 if step == 1 else 127
        rolled = jnp.where(lane == edge, 0.0, pltpu.roll(v, step % 128, 1))
        return jnp.where(wrap, rolled, v)

    wraps = [d <= 1] + [d == 0] * 4 + [None] * 4 + [d == ND - 1] * 4 + [d >= ND - 2]

    def placed(v, i):
        if i < 5:
            return shifted(v, wraps[i], 1)
        if i > 8:
            return shifted(v, wraps[i], -1)
        return v

    inv = []
    for c in range(2):
        inv.append([placed(jnp.broadcast_to(dwin[c, i : i + 1, :], (8, 128)), i) for i in range(14)])

    for c in ex4:
        c.wait_recv()

    both = mp[f]
    for i in range(1, NF):
        both = both + rb[field_at(i)].astype(F32)
    to_last = sum(xr4[0, g].astype(F32) for g in range(NF))
    to_first = sum(xr4[1, g].astype(F32) for g in range(NF))
    both = jnp.concatenate(
        [
            both[:, 0:128] + unpacked_rim(to_first, 0),
            both[:, 128:384],
            both[:, 384:512] + unpacked_rim(to_last, 96),
        ],
        axis=1,
    )
    moved_rhs = dot(hi_lo(both), pm[...])
    rhs = moved_rhs[0:CK] + moved_rhs[CK : 2 * CK]
    vb[...] = rhs.astype(BF)

    ex5 = [
        send(vb.at[:, pl.ds(384, 128)], ll, far[0]),
        send(vb.at[:, pl.ds(0, 128)], rr, far[1]),
        send(vb, ln, (dom_at(1), f)),
        send(vb, rn, (dom_at(-1), f)),
    ]
    for c in sent[:-4]:
        c.wait_send()
    for c in range(2):
        mixed_ref[c] = both[c * 32 : c * 32 + NFD]
    for c in ex5:
        c.wait_recv()

    corr = []
    for b in range(8):
        rows = slice(b * 8, b * 8 + 8)
        iv = inv[b // 4]
        pair = slice((b // 2) * 16, (b // 2) * 16 + 16)
        half = slice((b % 2) * 8, (b % 2) * 8 + 8)

        def get(ref, q):
            return ref[pair, q * 128 : (q + 1) * 128].astype(F32)[half]

        r = [get(ll, 0)] + [get(ln, q) for q in range(4)] + [rhs[rows, q * 128 : (q + 1) * 128] for q in range(4)]
        r = r + [get(rn, q) for q in range(4)] + [get(rr, 0)]
        yv = {i: iv[i] * placed(r[i], i) for i in range(14)}

        def residual(yy, zz, lo, hi):
            return {i: yy[i] + iv[i] * (zz[i - 1] + zz[i + 1]) - zz[i] for i in range(lo, hi)}

        def sweep(yy, lo, hi):
            step = dict(yy)
            total = dict(yy)
            rho = RHO0
            for _ in range(2):
                lo, hi = lo + 1, hi - 1
                rho_next = 1.0 / (2.0 * RATIO - rho)
                u = residual(yy, total, lo, hi)
                step = {i: (rho_next * rho) * step[i] + (2.0 * rho_next / HALF) * u[i] for i in range(lo, hi)}
                total = {i: total[i] + step[i] for i in range(lo, hi)}
                rho = rho_next
            return total, lo, hi

        first, lo, hi = sweep(yv, 0, 14)
        y2 = residual(yv, first, lo + 1, hi - 1)
        second, lo, hi = sweep(y2, lo + 1, hi - 1)
        corr.append(jnp.concatenate([first[i] + second[i] for i in range(5, 9)], axis=1))
    corr = jnp.concatenate(corr, axis=0)
    back = dot_nt(hi_lo(corr), pm[...])
    new = own32[...] - (back[0:CK] + back[CK : 2 * CK])
    for c in range(2):
        new_ref[c] = new[c * 32 : c * 32 + NFD]
    for c in ex5:
        c.wait_send()


def turn(new_ref, mixed_ref, new_out, mixed_out):
    for c in range(2):
        new_out[:, c, :] = new_ref[c]
        mixed_out[:, c, :] = mixed_ref[c]


def shards(
    traces,
    interior_source,
    orders,
    element_scale,
    element_faces,
    solver_slots,
    line_diagonal,
    species_mix,
    couple_in,
    local_inverse,
    trace_block,
    couple_out,
):
    vmem = pl.BlockSpec(memory_space=pltpu.VMEM)
    hbm = pl.BlockSpec(memory_space=pltpu.HBM)
    n_copies = 64
    scratch = [
        pltpu.VMEM((NF, CK, EXT), BF),
        pltpu.VMEM((EXT, 1024), BF),
        pltpu.VMEM((2, 1024, HE), BF),
        pltpu.VMEM((168, 896), BF),
        pltpu.VMEM((168, 672), BF),
        pltpu.VMEM((224, 896), BF),
        pltpu.VMEM((224, 672), BF),
        pltpu.VMEM((168, 1024), BF),
        pltpu.VMEM((168, PADK), BF),
        pltpu.VMEM((256, 1024), BF),
        pltpu.VMEM((NF, 256, 256), BF),
        pltpu.VMEM((NF, 256, 256), BF),
        pltpu.VMEM((168, ELEMS), F32),
        pltpu.VMEM((2, NF, 192, HE), BF),
        pltpu.VMEM((NF, CK, FACES), F32),
        pltpu.VMEM((NF, CK, FACES), BF),
        pltpu.VMEM((NF, CK, FACES), BF),
        pltpu.VMEM((2, 16, 128), BF),
        pltpu.VMEM((2, NF, 16, 128), BF),
        pltpu.VMEM((NF, 2, 16, 128), BF),
        pltpu.VMEM((2, NF, 16, 128), BF),
        pltpu.VMEM((CK, FACES), BF),
        pltpu.VMEM((CK, FACES), BF),
        pltpu.VMEM((CK, FACES), BF),
        pltpu.VMEM((CK, 128), BF),
        pltpu.VMEM((CK, 128), BF),
        pltpu.VMEM((8, 2, 128), F32),
        pltpu.VMEM((8, 2, 128), F32),
        pltpu.VMEM((8, 2, 8, 128), F32),
        pltpu.VMEM((2, 8, 2, 8, 128), F32),
        pltpu.VMEM((2, 128, 128), F32),
        pltpu.VMEM((2, 16, 128), F32),
        pltpu.VMEM((FACES, FACES), BF),
        pltpu.VMEM((CK, FACES), F32),
        pltpu.VMEM((2, 256, HE), F32),
        pltpu.VMEM((64, 8, 128), F32),
        pltpu.VMEM((2, FACES), F32),
        pltpu.VMEM((NFD, 2, FACES), F32),
        pltpu.VMEM((4, ELEMS), I32),
        pltpu.VMEM((1, ELEMS), I32),
        pltpu.VMEM((NID, 2, ELEMS), BF),
        pltpu.VMEM((1, FACES), I32),
        pltpu.VMEM((1, ELEMS), F32),
        pltpu.VMEM((NF, 2, 8), F32),
        pltpu.SemaphoreType.DMA((12,)),
        pltpu.SemaphoreType.DMA((n_copies,)),
        pltpu.SemaphoreType.DMA((n_copies,)),
    ]
    shape = jax.ShapeDtypeStruct((2, NFD, FACES), F32)
    new, mixed = pl.pallas_call(
        kernel,
        out_shape=(shape, shape),
        in_specs=[hbm] * 12,
        out_specs=(vmem, vmem),
        scratch_shapes=scratch,
        compiler_params=pltpu.CompilerParams(
            collective_id=0, has_side_effects=True, vmem_limit_bytes=48 * 1024 * 1024
        ),
    )(
        pltpu.with_memory_space_constraint(line_diagonal, pltpu.HBM),
        pltpu.with_memory_space_constraint(jnp.transpose(traces, (1, 0, 2)), pltpu.HBM),
        pltpu.with_memory_space_constraint(element_faces, pltpu.HBM),
        pltpu.with_memory_space_constraint(orders.reshape(1, ELEMS), pltpu.HBM),
        pltpu.with_memory_space_constraint(jnp.transpose(interior_source, (1, 0, 2)), pltpu.HBM),
        pltpu.with_memory_space_constraint(couple_in, pltpu.HBM),
        pltpu.with_memory_space_constraint(trace_block, pltpu.HBM),
        pltpu.with_memory_space_constraint(local_inverse, pltpu.HBM),
        pltpu.with_memory_space_constraint(couple_out, pltpu.HBM),
        pltpu.with_memory_space_constraint(solver_slots.reshape(1, FACES), pltpu.HBM),
        pltpu.with_memory_space_constraint(element_scale.reshape(1, ELEMS), pltpu.HBM),
        pltpu.with_memory_space_constraint(species_mix, pltpu.HBM),
    )
    turned = jax.ShapeDtypeStruct((NFD, 2, FACES), F32)
    new, mixed = pl.pallas_call(
        turn,
        out_shape=(turned, turned),
        in_specs=[vmem] * 2,
        out_specs=(vmem, vmem),
        compiler_params=pltpu.CompilerParams(vmem_limit_bytes=4 * 1024 * 1024),
    )(new, mixed)
    return jnp.transpose(new, (1, 0, 2)), jnp.transpose(mixed, (1, 0, 2))


def solution(mesh):
    in_specs = (
        P("field", None, "dom"),
        P("field", None, "dom"),
        P("dom"),
        P("dom"),
        P(None, "dom"),
        P("dom"),
        P("field", "dom"),
        P("field", None),
        P("field", None),
        P("field", None),
        P("field", None),
        P("field", None),
    )
    out_specs = (P("field", None, "dom"), P("field", None, "dom"))
    return jax.shard_map(shards, mesh=mesh, in_specs=in_specs, out_specs=out_specs, check_vma=False)
```

```python
import functools

import jax
import jax.numpy as jnp
from jax import lax
from jax.experimental import pallas as pl
from jax.experimental.pallas import tpu as pltpu
from jax.sharding import PartitionSpec as P

F32 = jnp.float32
BF = jnp.bfloat16
I32 = jnp.int32
MESH = pl.DeviceIdType.MESH

NFD = 28
NID = 84
ND = 128
NF = 4
FACES = 512
ELEMS = 256
CK = 64
EXT = 640
PADK = 768
HE = 128
RIM = 32
RHO0 = 0.8
HALF = 0.8
RATIO = 1.25


def dot(a, b):
    return jnp.dot(a, b, preferred_element_type=F32)


def dot_nt(a, b):
    return lax.dot_general(a, b, (((1,), (1,)), ((), ())), preferred_element_type=F32)


def iota(shape, dim):
    return lax.broadcasted_iota(I32, shape, dim)


def one_hot(cond):
    return jnp.where(cond, 1.0, 0.0).astype(BF)


def hi_lo(x):
    hi = x.astype(BF)
    lo = (x - hi.astype(F32)).astype(BF)
    return jnp.concatenate([hi, lo], axis=0)


def packed_rim(x, lane0):
    lane = iota((16, 128), 1)
    out = jnp.zeros((16, 128), F32)
    for i in range(4):
        part = pltpu.roll(x[16 * i : 16 * i + 16], (RIM * i - lane0) % 128, 1)
        out = jnp.where((lane >= RIM * i) & (lane < RIM * i + RIM), part, out)
    return out


def unpacked_rim(x, lane0):
    lane = iota((16, 128), 1)
    keep = (lane >= lane0) & (lane < lane0 + RIM)
    parts = [jnp.where(keep, pltpu.roll(x, (lane0 - RIM * i) % 128, 1), 0.0) for i in range(4)]
    return jnp.concatenate(parts, axis=0)


def kernel(
    dia_hbm, tr_hbm, fac_hbm, ord_hbm, src_hbm, ci_hbm, tb_hbm, li_hbm, co_hbm, slot_hbm, scl_hbm, mix_hbm,
    new_ref, mixed_ref,
    ta, oh, gat, civ, liv, tbv, cov, cip, lip, tbp, cop, cocol, srcf,
    lo_all, mp, sb, rb, rim1, xr1, rim4, xr4, vb, ln, rn, ll, rr,
    s1, r1, r2, r3, dt, dwin, pm, own32, tbg, cf,
    dia_ref, tr_ref, fac_ref, ord_ref, src_ref, slot_ref, scl_ref, mix_ref,
    wsem, ssem, rsem,
):
    d = lax.axis_index("dom")
    f = lax.axis_index("field")
    z = d // 16
    y = (d % 16) // 2
    k = d % 2

    def dom_at(step):
        return (d + step + ND) % ND

    def field_at(step):
        return (f + step) % NF

    pairs = (
        (tr_hbm, tr_ref), (dia_hbm, dia_ref), (fac_hbm, fac_ref), (ord_hbm, ord_ref), (src_hbm, src_ref),
        (ci_hbm, civ), (tb_hbm, tbv), (li_hbm, liv), (co_hbm, cov),
        (slot_hbm, slot_ref), (scl_hbm, scl_ref), (mix_hbm, mix_ref.at[f]),
    )
    fetch = [pltpu.make_async_copy(src, dst, wsem.at[i]) for i, (src, dst) in enumerate(pairs)]
    fetch[0].start()

    field_peers = [(d, field_at(i)) for i in range(1, NF)]
    far_first = [field_peers[1], field_peers[0], field_peers[2]]
    next_all = [(dom_at(1), field_at(i)) for i in range(NF)]
    prev_all = [(dom_at(-1), field_at(i)) for i in range(NF)]
    far = [(dom_at(2), f), (dom_at(-2), f)]
    z_peers = [(((z + i) % 8) * 16 + d % 16, f) for i in range(1, 8)]
    y_peers = [(z * 16 + ((y + i) % 8) * 2 + k, f) for i in range(1, 8)]
    core_peer = (d + 1 - 2 * k, f)
    hops = [side[i] for i in (2, 1, 3, 0) for side in (next_all, prev_all)]
    greet = hops + far_first + far + z_peers + y_peers
    barrier = pltpu.get_barrier_semaphore()
    for dev in greet:
        pl.semaphore_signal(barrier, inc=1, device_id=dev, device_id_type=MESH)
    for c in fetch[1:]:
        c.start()

    count = [0]
    sent = []

    def send(src, dst, dev):
        n = count[0]
        count[0] += 1
        c = pltpu.make_async_remote_copy(
            src_ref=src, dst_ref=dst, send_sem=ssem.at[n], recv_sem=rsem.at[n],
            device_id=dev, device_id_type=MESH,
        )
        c.start()
        sent.append(c)
        return c

    pad16 = jnp.zeros((16, HE), BF)
    for g in range(NF):
        for h in range(2):
            lo_all[h, g, 176:192, :] = pad16

    own32[...] = jnp.zeros((CK, FACES), F32)
    fetch[0].wait()
    for c in range(2):
        own32[c * 32 : c * 32 + NFD, :] = tr_ref[:, c, :]
    ta[f, :, 0:FACES] = own32[...].astype(BF)
    rim1[0] = packed_rim(own32[:, 0:128], 0).astype(BF)
    rim1[1] = packed_rim(own32[:, 384:512], 96).astype(BF)
    pl.semaphore_wait(barrier, len(greet))

    ex1 = []
    for i in (2, 1, 3, 0):
        ex1.append(send(rim1.at[1], xr1.at[0, f], next_all[i]))
        ex1.append(send(rim1.at[0], xr1.at[1, f], prev_all[i]))
    for dev in far_first:
        ex1.append(send(ta.at[f, :, pl.ds(0, FACES)], ta.at[f, :, pl.ds(0, FACES)], dev))
    fetch[11].wait()
    exm = [send(mix_ref.at[f], mix_ref.at[f], dev) for dev in field_peers]
    fetch[1].wait()
    dia = jnp.concatenate([dia_ref[...]] * 4, axis=0)
    for zz in range(8):
        s1[zz] = pltpu.roll(dia, (8 - 64 * zz) % FACES, 1)[0:2, 0:128]
    dz = []
    for i in range(1, 8):
        dz.append(send(s1.at[(z + i) % 8], r1.at[z], z_peers[i - 1]))
    r1[z] = s1[z]

    rown = iota((256, 224), 0)
    rk = rown & 31
    want_r = jnp.where(rk < NFD, ((rown >> 5) & 1) * 112 + (rown >> 6) * NFD + rk, -1)
    permr = one_hot(iota((256, 224), 1) == want_r)
    colw = iota((672, 1024), 1)
    inn = colw & 255
    permw = one_hot(iota((672, 1024), 0) == jnp.where(inn < 168, (colw >> 8) * 168 + inn, -1))
    fetch[8].wait()
    wide = dot(dot(permr, cov[...]).astype(BF), permw).astype(BF)
    for g in range(NF):
        cop[g] = wide[:, g * 256 : (g + 1) * 256]
    half_rows = pl.ds(pl.multiple_of(k * 128, 128), 128)
    exw = []
    for i in range(1, NF):
        exw.append(send(cop.at[field_at(i), half_rows], cocol.at[f, half_rows], field_peers[i - 1]))
    cocol[f] = cop[f]

    fetch[2].wait()
    rel = (fac_ref[...] - d * FACES) & (ND * FACES - 1)
    lid = jnp.where(
        rel < FACES, rel, jnp.where(rel >= ND * FACES - RIM, rel - (ND * FACES - RIM) + FACES, rel + RIM)
    )
    for h in range(2):
        for j in range(4):
            c0 = h * 512 + j * HE
            oh[:, c0 : c0 + HE] = one_hot(iota((EXT, HE), 0) == lid[j : j + 1, h * HE : h * HE + HE])
    fetch[3].wait()
    order = ord_ref[...]
    face_n = (order + 1) * (order + 2)
    inner_n = face_n * (order + 3)
    face_live = 2 * (iota((256, ELEMS), 0) & 31) < face_n
    row = iota((2 * NID, ELEMS), 0)
    inner_live = 6 * jnp.where(row >= NID, row - NID, row) < inner_n
    fetch[4].wait()
    for c in range(2):
        srcf[c * NID : (c + 1) * NID, :] = src_ref[:, c, :].astype(F32)
    zero8 = jnp.zeros((8, HE), F32)

    col = iota((896, 1024), 1)
    kk = col & 31
    want = jnp.where(kk < NFD, ((col >> 5) & 7) * 112 + (col >> 8) * NFD + kk, -1)
    permk = one_hot(iota((896, 1024), 0) == want)
    fetch[5].wait()
    cip[...] = dot(civ[...], permk).astype(BF)

    for c in ex1[0:8]:
        c.wait_recv()
    for g in range(NF):
        ta[g, :, FACES:EXT] = (
            unpacked_rim(xr1[0, g].astype(F32), 0) + unpacked_rim(xr1[1, g].astype(F32), RIM)
        ).astype(BF)
    for c in ex1[8:]:
        c.wait_recv()
    tall = ta[...].reshape(256, EXT)
    ex2 = [[], []]
    for h in range(2):
        es = slice(h * HE, h * HE + HE)
        picked = dot(tall, oh[:, h * 512 : h * 512 + 512])
        for j in range(4):
            live = jnp.where(face_live[:, es], picked[:, j * HE : (j + 1) * HE], 0.0)
            gat[h, j * 256 : (j + 1) * 256, :] = live.astype(BF)
        loads = srcf[:, es] - dot(cip[...], gat[h])
        loads = jnp.where(inner_live[:, es], loads, 0.0)
        lo_all[h, f, 0:176] = jnp.concatenate([loads, zero8], axis=0).astype(BF)
        for dev in far_first:
            ex2[h].append(send(lo_all.at[h, f, pl.ds(0, 176)], lo_all.at[h, f, pl.ds(0, 176)], dev))
    for c in exm:
        c.wait_recv()
    for c in range(8):
        for c2 in range(8):
            coef = mix_ref[c // 2, c % 2 : c % 2 + 1, c2 : c2 + 1] + (1.0 if c == c2 else 0.0)
            cf[c * 8 + c2] = jnp.broadcast_to(coef, (8, 128))
    for c in exw:
        c.wait_recv()
    exf = []
    for i in range(1, NF):
        part = cocol.at[field_at(i), half_rows]
        exf.append(send(part, part, core_peer))
    for c in dz:
        c.wait_recv()
    for c in range(2):
        r2[y, c] = r1[:, c, :]
    dy = []
    for i in range(1, 8):
        dy.append(send(r2.at[y], r2.at[y], y_peers[i - 1]))

    colw = iota((672, PADK), 1)
    slab = (colw >= 192).astype(I32) + (colw >= 384).astype(I32) + (colw >= 576).astype(I32)
    inn = colw - slab * 192
    perms = one_hot(iota((672, PADK), 0) == jnp.where(inn < 168, slab * 168 + inn, -1))
    fetch[7].wait()
    lip[...] = dot(liv[...], perms).astype(BF)
    fetch[6].wait()
    tbp[...] = dot(dot(permr, tbv[...]).astype(BF), permk).astype(BF)
    for h in range(2):
        tbg[h] = dot(tbp[...], gat[h])

    for c in exf:
        c.wait_recv()
    fetch[10].wait()
    zero88 = jnp.zeros((88, HE), F32)
    def mixed_share(part, c):
        total = None
        for c2 in range(8):
            coef = jnp.concatenate([cf[c * 8 + c2]] * 4, axis=0)
            coef = jnp.concatenate([coef] * (part.shape[1] // 128), axis=1)
            term = coef * part[c2 * 32 : c2 * 32 + 32]
            total = term if total is None else total + term
        return total

    flats = []
    for h in range(2):
        es = slice(h * HE, h * HE + HE)
        for c in ex2[h]:
            c.wait_recv()
        inter = dot(lip[...], lo_all[h].reshape(PADK, HE))
        inter = jnp.where(inner_live[:, es], inter, 0.0)
        inter = jnp.concatenate([inter, zero88], axis=0).astype(BF)
        his, los = [], []
        for g in range(NF):
            blocks = dot(cocol[g], inter) + jnp.where(f == g, tbg[h], 0.0)
            blocks = jnp.where(face_live[:, es], blocks, 0.0) * scl_ref[:, es]
            flat = jnp.concatenate([blocks[j * CK : (j + 1) * CK] for j in range(4)], axis=1)
            hi = flat.astype(BF)
            his.append(hi)
            los.append((flat - hi.astype(F32)).astype(BF))
        flats.append(jnp.concatenate(his + los, axis=0))
        if h == 0:
            rim_part = dot_nt(flats[0], oh[FACES:EXT, 0:512])
            acc_part = dot_nt(flats[0], oh[0:FACES, 0:512])

    rim_part = rim_part + dot_nt(flats[1], oh[FACES:EXT, 512:1024])
    rim_part = rim_part[0:256] + rim_part[256:512]
    for g in range(NF):
        rim = jnp.concatenate([mixed_share(rim_part, 2 * g), mixed_share(rim_part, 2 * g + 1)], axis=0)
        rim4[g, 0] = packed_rim(rim, 0).astype(BF)
        rim4[g, 1] = packed_rim(rim, RIM).astype(BF)

    ex4 = []
    for i in (2, 1, 3, 0):
        ex4.append(send(rim4.at[field_at(i), 0], xr4.at[0, f], prev_all[i]))
        ex4.append(send(rim4.at[field_at(i), 1], xr4.at[1, f], next_all[i]))
    acc_part = acc_part + dot_nt(flats[1], oh[0:FACES, 512:1024])
    acc_part = acc_part[0:256] + acc_part[256:512]
    for g in range(NF):
        own = jnp.concatenate([mixed_share(acc_part, 2 * g), mixed_share(acc_part, 2 * g + 1)], axis=0)
        mp[g] = own
        sb[g] = own.astype(BF)
    for i in (2, 1, 3):
        ex4.append(send(sb.at[field_at(i)], rb.at[f], field_peers[i - 1]))

    for c in dy:
        c.wait_recv()
    dk = send(r2, r3.at[k], core_peer)
    r3[k] = r2[...]

    fetch[9].wait()
    slots = slot_ref[...]
    parts = jnp.concatenate([(slots >> 4).astype(F32), (slots & 15).astype(F32)] + [jnp.zeros((6, FACES), F32)], axis=0)
    cs = iota((FACES, FACES), 1)
    spread = one_hot(iota((FACES, FACES), 0) == (cs & 127) * 4 + (cs >> 7))
    moved = dot(parts.astype(BF), spread).astype(I32)
    slot_qt = moved[0:1] * 16 + moved[1:2]
    pm[...] = one_hot(iota((FACES, FACES), 0) == slot_qt)

    dk.wait_recv()
    r_i = iota((128, 128), 0)
    t_of = (r_i & 7) * 16 + ((r_i >> 3) & 7) * 2 + (r_i >> 6)
    to_t = one_hot(iota((128, 128), 1) == t_of)
    for c in range(2):
        dt[c] = r3[:, :, c].reshape(128, 128).T
    start = 3 + 4 * (d % 16)
    lane = iota((1, 128), 1)
    for c in range(2):
        win = dt[c, pl.ds(start, 16), :]
        w0 = win.astype(BF)
        rest = win - w0.astype(F32)
        w1 = rest.astype(BF)
        w2 = (rest - w1.astype(F32)).astype(BF)
        got = dot(jnp.concatenate([w0, w1, w2], axis=0), to_t)
        dwin[c] = 1.0 / (got[0:16] + got[16:32] + got[32:48])

    def shifted(v, wrap, step):
        edge = 0 if step == 1 else 127
        rolled = jnp.where(lane == edge, 0.0, pltpu.roll(v, step % 128, 1))
        return jnp.where(wrap, rolled, v)

    wraps = [d <= 1] + [d == 0] * 4 + [None] * 4 + [d == ND - 1] * 4 + [d >= ND - 2]

    def placed(v, i):
        if i < 5:
            return shifted(v, wraps[i], 1)
        if i > 8:
            return shifted(v, wraps[i], -1)
        return v

    inv = []
    for c in range(2):
        inv.append([placed(jnp.broadcast_to(dwin[c, i : i + 1, :], (8, 128)), i) for i in range(14)])

    for c in ex4:
        c.wait_recv()

    both = mp[f]
    for i in range(1, NF):
        both = both + rb[field_at(i)].astype(F32)
    to_last = sum(xr4[0, g].astype(F32) for g in range(NF))
    to_first = sum(xr4[1, g].astype(F32) for g in range(NF))
    both = jnp.concatenate(
        [
            both[:, 0:128] + unpacked_rim(to_first, 0),
            both[:, 128:384],
            both[:, 384:512] + unpacked_rim(to_last, 96),
        ],
        axis=1,
    )
    moved_rhs = dot(hi_lo(both), pm[...])
    rhs = moved_rhs[0:CK] + moved_rhs[CK : 2 * CK]
    vb[...] = rhs.astype(BF)

    ex5 = [
        send(vb.at[:, pl.ds(384, 128)], ll, far[0]),
        send(vb.at[:, pl.ds(0, 128)], rr, far[1]),
        send(vb, ln, (dom_at(1), f)),
        send(vb, rn, (dom_at(-1), f)),
    ]
    for c in sent[:-4]:
        c.wait_send()
    for c in range(2):
        mixed_ref[c] = both[c * 32 : c * 32 + NFD]
    for c in ex5:
        c.wait_recv()

    corr = []
    for b in range(8):
        rows = slice(b * 8, b * 8 + 8)
        iv = inv[b // 4]
        pair = slice((b // 2) * 16, (b // 2) * 16 + 16)
        half = slice((b % 2) * 8, (b % 2) * 8 + 8)

        def get(ref, q):
            return ref[pair, q * 128 : (q + 1) * 128].astype(F32)[half]

        r = [get(ll, 0)] + [get(ln, q) for q in range(4)] + [rhs[rows, q * 128 : (q + 1) * 128] for q in range(4)]
        r = r + [get(rn, q) for q in range(4)] + [get(rr, 0)]
        yv = {i: iv[i] * placed(r[i], i) for i in range(14)}

        def residual(yy, zz, lo, hi):
            return {i: yy[i] + iv[i] * (zz[i - 1] + zz[i + 1]) - zz[i] for i in range(lo, hi)}

        def sweep(yy, lo, hi):
            step = dict(yy)
            total = dict(yy)
            rho = RHO0
            for _ in range(2):
                lo, hi = lo + 1, hi - 1
                rho_next = 1.0 / (2.0 * RATIO - rho)
                u = residual(yy, total, lo, hi)
                step = {i: (rho_next * rho) * step[i] + (2.0 * rho_next / HALF) * u[i] for i in range(lo, hi)}
                total = {i: total[i] + step[i] for i in range(lo, hi)}
                rho = rho_next
            return total, lo, hi

        first, lo, hi = sweep(yv, 0, 14)
        y2 = residual(yv, first, lo + 1, hi - 1)
        second, lo, hi = sweep(y2, lo + 1, hi - 1)
        corr.append(jnp.concatenate([first[i] + second[i] for i in range(5, 9)], axis=1))
    corr = jnp.concatenate(corr, axis=0)
    back = dot_nt(hi_lo(corr), pm[...])
    new = own32[...] - (back[0:CK] + back[CK : 2 * CK])
    for c in range(2):
        new_ref[c] = new[c * 32 : c * 32 + NFD]
    for c in ex5:
        c.wait_send()


def turn(new_ref, mixed_ref, new_out, mixed_out):
    for c in range(2):
        new_out[:, c, :] = new_ref[c]
        mixed_out[:, c, :] = mixed_ref[c]


def shards(
    traces,
    interior_source,
    orders,
    element_scale,
    element_faces,
    solver_slots,
    line_diagonal,
    species_mix,
    couple_in,
    local_inverse,
    trace_block,
    couple_out,
):
    vmem = pl.BlockSpec(memory_space=pltpu.VMEM)
    hbm = pl.BlockSpec(memory_space=pltpu.HBM)
    n_copies = 64
    scratch = [
        pltpu.VMEM((NF, CK, EXT), BF),
        pltpu.VMEM((EXT, 1024), BF),
        pltpu.VMEM((2, 1024, HE), BF),
        pltpu.VMEM((168, 896), BF),
        pltpu.VMEM((168, 672), BF),
        pltpu.VMEM((224, 896), BF),
        pltpu.VMEM((224, 672), BF),
        pltpu.VMEM((168, 1024), BF),
        pltpu.VMEM((168, PADK), BF),
        pltpu.VMEM((256, 1024), BF),
        pltpu.VMEM((NF, 256, 256), BF),
        pltpu.VMEM((NF, 256, 256), BF),
        pltpu.VMEM((168, ELEMS), F32),
        pltpu.VMEM((2, NF, 192, HE), BF),
        pltpu.VMEM((NF, CK, FACES), F32),
        pltpu.VMEM((NF, CK, FACES), BF),
        pltpu.VMEM((NF, CK, FACES), BF),
        pltpu.VMEM((2, 16, 128), BF),
        pltpu.VMEM((2, NF, 16, 128), BF),
        pltpu.VMEM((NF, 2, 16, 128), BF),
        pltpu.VMEM((2, NF, 16, 128), BF),
        pltpu.VMEM((CK, FACES), BF),
        pltpu.VMEM((CK, FACES), BF),
        pltpu.VMEM((CK, FACES), BF),
        pltpu.VMEM((CK, 128), BF),
        pltpu.VMEM((CK, 128), BF),
        pltpu.VMEM((8, 2, 128), F32),
        pltpu.VMEM((8, 2, 128), F32),
        pltpu.VMEM((8, 2, 8, 128), F32),
        pltpu.VMEM((2, 8, 2, 8, 128), F32),
        pltpu.VMEM((2, 128, 128), F32),
        pltpu.VMEM((2, 16, 128), F32),
        pltpu.VMEM((FACES, FACES), BF),
        pltpu.VMEM((CK, FACES), F32),
        pltpu.VMEM((2, 256, HE), F32),
        pltpu.VMEM((64, 8, 128), F32),
        pltpu.VMEM((2, FACES), F32),
        pltpu.VMEM((NFD, 2, FACES), F32),
        pltpu.VMEM((4, ELEMS), I32),
        pltpu.VMEM((1, ELEMS), I32),
        pltpu.VMEM((NID, 2, ELEMS), BF),
        pltpu.VMEM((1, FACES), I32),
        pltpu.VMEM((1, ELEMS), F32),
        pltpu.VMEM((NF, 2, 8), F32),
        pltpu.SemaphoreType.DMA((12,)),
        pltpu.SemaphoreType.DMA((n_copies,)),
        pltpu.SemaphoreType.DMA((n_copies,)),
    ]
    shape = jax.ShapeDtypeStruct((2, NFD, FACES), F32)
    new, mixed = pl.pallas_call(
        kernel,
        out_shape=(shape, shape),
        in_specs=[hbm] * 12,
        out_specs=(vmem, vmem),
        scratch_shapes=scratch,
        compiler_params=pltpu.CompilerParams(
            collective_id=0, has_side_effects=True, vmem_limit_bytes=48 * 1024 * 1024
        ),
    )(
        pltpu.with_memory_space_constraint(line_diagonal, pltpu.HBM),
        pltpu.with_memory_space_constraint(jnp.transpose(traces, (1, 0, 2)), pltpu.HBM),
        pltpu.with_memory_space_constraint(element_faces, pltpu.HBM),
        pltpu.with_memory_space_constraint(orders.reshape(1, ELEMS), pltpu.HBM),
        pltpu.with_memory_space_constraint(jnp.transpose(interior_source, (1, 0, 2)), pltpu.HBM),
        pltpu.with_memory_space_constraint(couple_in, pltpu.HBM),
        pltpu.with_memory_space_constraint(trace_block, pltpu.HBM),
        pltpu.with_memory_space_constraint(local_inverse, pltpu.HBM),
        pltpu.with_memory_space_constraint(couple_out, pltpu.HBM),
        pltpu.with_memory_space_constraint(solver_slots.reshape(1, FACES), pltpu.HBM),
        pltpu.with_memory_space_constraint(element_scale.reshape(1, ELEMS), pltpu.HBM),
        pltpu.with_memory_space_constraint(species_mix, pltpu.HBM),
    )
    turned = jax.ShapeDtypeStruct((NFD, 2, FACES), F32)
    new, mixed = pl.pallas_call(
        turn,
        out_shape=(turned, turned),
        in_specs=[vmem] * 2,
        out_specs=(vmem, vmem),
        compiler_params=pltpu.CompilerParams(vmem_limit_bytes=4 * 1024 * 1024),
    )(new, mixed)
    return jnp.transpose(new, (1, 0, 2)), jnp.transpose(mixed, (1, 0, 2))


def solution(mesh):
    in_specs = (
        P("field", None, "dom"),
        P("field", None, "dom"),
        P("dom"),
        P("dom"),
        P(None, "dom"),
        P("dom"),
        P("field", "dom"),
        P("field", None),
        P("field", None),
        P("field", None),
        P("field", None),
        P("field", None),
    )
    out_specs = (P("field", None, "dom"), P("field", None, "dom"))
    return jax.shard_map(shards, mesh=mesh, in_specs=in_specs, out_specs=out_specs, check_vma=False)
```
